32 devices in a mesh: tok: 4 (over z), head: 8 (over y, x, core).
Axes of the slice: x: 2, y: 2, z: 4, core: 2. Of those that a mesh axis runs over, the one named last changes fastest.
Arguments:
- block_states: bfloat16 [1024, 2048], P('tok', 'head'), may hold values from -24 to 24
- token_ids: int32 [1024], replicated, may hold values from 0 to 100351
- accept: int32 [1024], P('tok'), may hold values 0 or 1
- cache_lengths: int32 [4], replicated, may hold values from 1 to 3072, as said below
- cache_keys: bfloat16 [4096, 2048], P('tok', 'head'), may hold values from -300 to 300
- cache_values: bfloat16 [4096, 2048], P('tok', 'head'), may hold values from -6 to 6
- w_query: bfloat16 [2048, 2048], P(None, 'head'), may hold values from -0.125 to 0.125
- w_key: bfloat16 [2048, 2048], P(None, 'head'), may hold values from -0.125 to 0.125
- w_value: bfloat16 [2048, 2048], P(None, 'head'), may hold values from -0.125 to 0.125
- w_out: bfloat16 [2048, 2048], P('head'), may hold values from -0.125 to 0.125
- attn_gain: float32 [2048], replicated, may hold values from 0.25 to 1.75
- final_gain: float32 [2048], replicated, may hold values from 0.25 to 1.75
- embed: bfloat16 [100352, 2048], P('tok', 'head'), may hold values from -6 to 6
- lm_head: bfloat16 [100352, 2048], P(('tok', 'head')), may hold values from -0.25 to 0.25
Outputs:
- hiddens: bfloat16 [1024, 2048], P(('tok', 'head'))
- request_norms: float32 [4], replicated
- top_logits: float32 [1024], replicated
The draws below stay inside these ranges and needn't reach their ends.
Inputs may be any that keep to these rules, and one draw needn't show every extreme that they name: `cache_lengths`: each request has 1 or more cached positions; the counts sum to 4096 and the largest is exactly 3072.
All inputs are finite; a program needn't handle non-finite values. No bound on the sum of `accept` on one device may be relied on, other than what follows from the above.
Results may differ from the reference program's by a relative error of at most 0.0068.
Values may be sent and summed in bfloat16 or wider, within the bound.
No kernel may reach another device: no remote copies, remote signals or barrier semaphores. Data moves between devices by JAX's collectives and lax.ppermute only.
A program may use at most 192 MiB of HBM per device.

```python
import math
import jax
import jax.numpy as jnp
import numpy as np
from jax import lax

HEAD_DIM = 128
HEADS = 16
D = 2048
VOCAB = 100352
BLOCK = 256
REQS = 4
ROWS = 1024
CACHE_DEV = 1024
CACHE = 4096
LONGEST = 3072
N_TOK = 4
N_HEAD = 8


def draw_block_states(key, part):
    first_key, second_key = jax.random.split(key, 2)
    positions = (jnp.arange(ROWS) % BLOCK).astype(jnp.float32) / BLOCK
    jitter = jax.random.uniform(second_key, (ROWS, 1), jnp.float32, 0.7, 1.3)
    base_draw = jnp.clip(jax.random.normal(first_key, (ROWS, D), jnp.float32), -4.0, 4.0)
    scaled = base_draw * jnp.exp(1.2 * positions)[:, None] * jitter
    return jnp.clip(scaled, -24.0, 24.0).astype(jnp.bfloat16)


def draw_cache_keys(key, part):
    first_key = jax.random.fold_in(key, 0)
    values = jnp.clip(jax.random.normal(first_key, (CACHE, D), jnp.float32), -5.0, 5.0)
    return values.astype(jnp.bfloat16)


def draw_cache_lengths(key, part):
    first_key, second_key, third_key = jax.random.split(jax.random.fold_in(key, 17), 3)
    long_index = jax.random.randint(first_key, (), REQS // 2, REQS - 1).astype(jnp.int32)
    index = jnp.arange(REQS, dtype=jnp.int32)
    before_draw = jax.random.randint(second_key, (REQS,), 1, CACHE_DEV // REQS + 1).astype(jnp.int32)
    before = jnp.where(index < long_index, before_draw, 0).astype(jnp.int32)
    rest = ((REQS // 2 - 1) * CACHE_DEV - jnp.sum(before)).astype(jnp.int32)
    after_mask = index > long_index
    after_count = (REQS - 1 - long_index).astype(jnp.int32)
    weights = jnp.where(after_mask, jax.random.randint(third_key, (REQS,), 1, 101), 0).astype(jnp.int32)
    extra = rest - after_count
    share = extra * weights // jnp.sum(weights)
    remainder = extra - jnp.sum(share)
    after = jnp.where(after_mask, 1 + share, 0) + jnp.where(index == REQS - 1, remainder, 0)
    total = before + after + jnp.where(index == long_index, LONGEST, 0)
    return total.astype(jnp.int32)


def set_ends(array, own_key, least, top_value):
    longest = array.shape.index(max(array.shape))
    spots = []
    for shift in (0, 1):
        where = [jax.random.randint(jax.random.fold_in(own_key, axis), (), 0, length) for axis, length in enumerate(array.shape)]
        where[longest] = (where[longest] + shift) % array.shape[longest]
        spots.append(tuple(where))
    return array.at[spots[0]].set(least).at[spots[1]].set(top_value)


def levels(rng, dims, pieces, smallest, high):
    gain, own = 1.0, jax.random.fold_in(rng, 6)
    for axis_at, shards_of in pieces:
        draws = jnp.exp(jax.random.uniform(jax.random.fold_in(own, axis_at), (shards_of,), jnp.float32, smallest / len(pieces), high / len(pieces)))
        gain = gain * jnp.repeat(draws, dims[axis_at] // shards_of).reshape([-1 if axis == axis_at else 1 for axis in range(len(dims))])
    return gain


def wide_ids(key, dims, count, slope):
    weights = [min(1 << octave, count + 1 - (1 << octave)) * (1 << 20) // math.isqrt((1 << octave) ** slope) + 1 for octave in range((count + 1).bit_length()) if 1 << octave <= count]
    spread = 1 + sum(weights) // (1 << 30)
    grid = np.cumsum(np.array([max(1, weight // spread) for weight in weights]))
    lot = jax.random.randint(jax.random.fold_in(key, 1), dims, 0, int(grid[len(weights) - 1]))
    start = jnp.left_shift(1, jnp.searchsorted(jnp.asarray(grid, jnp.int32), lot, side="right").astype(jnp.int32))
    standing = start - 1 + jax.random.randint(jax.random.fold_in(key, 4), dims, 0, 1 << 30) % jnp.minimum(start, count + 1 - start)
    return jax.random.permutation(jax.random.fold_in(key, 2), count)[standing].astype(jnp.int32)


def centred(key, extent, scale, most, cuts=(), kind=jnp.bfloat16):
    loudness = levels(key, extent, cuts, -0.22, 0.18) if cuts else 1.0
    entries = jax.random.normal(key, extent, jnp.float32) * scale * loudness
    return jnp.minimum(jnp.maximum(entries, -most), most).astype(kind)


def setup_inputs(seed: int = 0) -> dict:
    seeds = jax.random.split(jax.random.key(seed), 15)
    return {
        "block_states": draw_block_states(jax.random.fold_in(seeds[14], 71), 0),
        "token_ids": set_ends(wide_ids(seeds[1], (ROWS,), VOCAB, 2), jax.random.fold_in(seeds[1], 3), 0, VOCAB - 1).astype(jnp.int32),
        "accept": set_ends((jax.random.randint(seeds[2], (ROWS,), 0, 3) < 1).astype(jnp.int32), jax.random.fold_in(seeds[2], 1), 0, 1),
        "cache_lengths": draw_cache_lengths(jax.random.fold_in(seeds[14], 71), 0),
        "cache_keys": draw_cache_keys(jax.random.fold_in(seeds[14], 71), 0),
        "cache_values": centred(seeds[5], (CACHE, D), 1.0, 6.0, ((0, 4), (1, 8))),
        "w_query": centred(seeds[6], (D, D), D ** -0.5, 0.125, ((1, 8),)),
        "w_key": centred(seeds[7], (D, D), D ** -0.5, 0.125, ((1, 8),)),
        "w_value": centred(seeds[8], (D, D), D ** -0.5, 0.125, ((1, 8),)),
        "w_out": centred(seeds[9], (D, D), D ** -0.5, 0.125, ((0, 8),)),
        "attn_gain": jnp.clip(1.0 + 0.15 * jax.random.normal(seeds[10], (D,), jnp.float32), 0.25, 1.75),
        "final_gain": jnp.clip(1.0 + 0.15 * jax.random.normal(seeds[11], (D,), jnp.float32), 0.25, 1.75),
        "embed": centred(seeds[12], (VOCAB, D), 1.0, 6.0, ((0, 4), (1, 8))),
        "lm_head": centred(seeds[13], (VOCAB, D), 0.046875, 0.25, ((0, 32),)),
    }


EPSILON = 1e-06

def row_norm(values):
    return values * lax.rsqrt(lax.optimization_barrier(jnp.mean(values * values, axis=-1, keepdims=True)) + EPSILON)

def run_layer(inputs, offsets, counts, cache_keys, cache_values, w_query, w_key, w_value, w_out, attn_gain):
    queries = jnp.dot(inputs, w_query, preferred_element_type=jnp.float32).astype(jnp.bfloat16)
    new_keys = jnp.dot(inputs, w_key, preferred_element_type=jnp.float32).astype(jnp.bfloat16)
    new_values = jnp.dot(inputs, w_value, preferred_element_type=jnp.float32).astype(jnp.bfloat16)
    padding = jnp.zeros((LONGEST, D), jnp.bfloat16)
    padded_keys = jnp.concatenate([cache_keys, padding], axis=0)
    padded_values = jnp.concatenate([cache_values, padding], axis=0)
    score_scale = 1.0 / math.sqrt(HEAD_DIM)

    def one_request(request):
        row_start = (request * BLOCK).astype(jnp.int32)
        query_heads = lax.dynamic_slice_in_dim(queries, row_start, BLOCK, 0).astype(jnp.float32).reshape(BLOCK, HEADS, HEAD_DIM)
        block_keys = lax.dynamic_slice_in_dim(new_keys, row_start, BLOCK, 0).astype(jnp.float32).reshape(BLOCK, HEADS, HEAD_DIM)
        block_values = lax.dynamic_slice_in_dim(new_values, row_start, BLOCK, 0).astype(jnp.float32).reshape(BLOCK, HEADS, HEAD_DIM)
        cache_start = offsets[request].astype(jnp.int32)
        cached_keys = lax.dynamic_slice_in_dim(padded_keys, cache_start, LONGEST, 0).astype(jnp.float32).reshape(LONGEST, HEADS, HEAD_DIM)
        cached_values = lax.dynamic_slice_in_dim(padded_values, cache_start, LONGEST, 0).astype(jnp.float32).reshape(LONGEST, HEADS, HEAD_DIM)
        valid_keys = jnp.arange(LONGEST, dtype=jnp.int32) < counts[request]
        cache_scores = jnp.einsum('qhd,khd->hqk', query_heads, cached_keys) * score_scale
        cache_scores = jnp.where(valid_keys[None, None, :], cache_scores, -jnp.inf)
        block_scores = jnp.einsum('qhd,khd->hqk', query_heads, block_keys) * score_scale
        largest = jnp.maximum(lax.optimization_barrier(jnp.max(cache_scores, axis=-1)), lax.optimization_barrier(jnp.max(block_scores, axis=-1)))
        cache_weights = jnp.exp(cache_scores - largest[:, :, None])
        block_weights = jnp.exp(block_scores - largest[:, :, None])
        weight_sum = lax.optimization_barrier(jnp.sum(cache_weights, axis=-1)) + lax.optimization_barrier(jnp.sum(block_weights, axis=-1))
        mixed = jnp.einsum('hqk,khd->qhd', cache_weights, cached_values) + jnp.einsum('hqk,khd->qhd', block_weights, block_values)
        mixed = mixed / jnp.transpose(weight_sum)[:, :, None]
        return mixed.reshape(BLOCK, D).astype(jnp.bfloat16)
    attended = lax.map(one_request, jnp.arange(REQS, dtype=jnp.int32)).reshape(ROWS, D)
    projected = jnp.dot(attended, w_out, preferred_element_type=jnp.float32)
    return (inputs.astype(jnp.float32) + row_norm(projected) * attn_gain).astype(jnp.bfloat16)

def reference(block_states, token_ids, accept, cache_lengths, cache_keys, cache_values, w_query, w_key, w_value, w_out, attn_gain, final_gain, embed, lm_head):
    counts = cache_lengths.astype(jnp.int32)
    offsets = (jnp.cumsum(counts) - counts).astype(jnp.int32)
    first_pass = run_layer(block_states, offsets, counts, cache_keys, cache_values, w_query, w_key, w_value, w_out, attn_gain)
    widened = first_pass.astype(jnp.float32)
    request_norms = jnp.sqrt(lax.optimization_barrier(jnp.mean((widened * widened).reshape(REQS, BLOCK * D), axis=1)))
    normed = (row_norm(widened) * final_gain).astype(jnp.bfloat16)
    shards = N_TOK * N_HEAD
    vocab_pieces = lm_head.reshape(shards, VOCAB // shards, D)

    def piece_max(vocab_piece):
        logits = lax.dot_general(normed, vocab_piece, (((1,), (1,)), ((), ())), preferred_element_type=jnp.float32)
        return lax.optimization_barrier(jnp.max(logits, axis=1))
    top_logits = lax.optimization_barrier(jnp.max(lax.map(piece_max, vocab_pieces), axis=0))
    chosen = (accept == 1)[:, None]
    swapped = jnp.where(chosen, embed[token_ids], block_states)
    hiddens = run_layer(swapped, offsets, counts, cache_keys, cache_values, w_query, w_key, w_value, w_out, attn_gain)
    return (hiddens, request_norms, top_logits)
```

```python
import functools
import math

import jax
import jax.numpy as jnp
from jax import lax
from jax.experimental import pallas as pl
from jax.experimental.pallas import tpu as pltpu
from jax.sharding import PartitionSpec as P

HEAD_DIM = 128
EPSILON = 1e-06
LOWEST = -1e30
BF16 = jnp.bfloat16
F32 = jnp.float32

SMEM = pl.BlockSpec(memory_space=pltpu.SMEM)
VMEM = pl.BlockSpec(memory_space=pltpu.VMEM)


def params(mib=48):
    return pltpu.CompilerParams(vmem_limit_bytes=mib * 2**20)


def cost(flops, moved):
    return pl.CostEstimate(flops=flops, bytes_accessed=moved, transcendentals=0)


def xor_pairs(size, mask):
    return [(i, i ^ mask) for i in range(size)]


def project_kernel(place, *refs):
    *pieces, wq, wk, wv, q_out, k_out, v_out, res_out, x = refs
    head = place[1]
    width = pieces[0].shape[1]
    for mask, piece in enumerate(pieces):
        at = pl.multiple_of(jnp.bitwise_xor(head, mask) * width, width)
        x[:, pl.ds(at, width)] = piece[...]
    for w, out in ((wq, q_out), (wk, k_out), (wv, v_out)):
        out[...] = jnp.dot(x[...], w[...], preferred_element_type=F32).astype(BF16)
    share = res_out.shape[0]
    res_out[...] = x[pl.ds(pl.multiple_of(head * share, share), share), :]


def project(place, pieces, wq, wk, wv):
    rows, width = pieces[0].shape
    full = wq.shape[0]
    share = rows // len(pieces)
    tile = jax.ShapeDtypeStruct((rows, width), BF16)
    return pl.pallas_call(
        project_kernel,
        out_shape=(tile, tile, tile, jax.ShapeDtypeStruct((share, full), BF16)),
        in_specs=[SMEM] + [VMEM] * (len(pieces) + 3),
        out_specs=(VMEM,) * 4,
        scratch_shapes=[pltpu.VMEM((rows, full), BF16)],
        compiler_params=params(),
        cost_estimate=cost(6 * rows * full * width, 8 * full * width),
        name="project",
    )(place, *pieces, wq, wk, wv)


def key_range(place, request, chunk_rows, tok_count):
    begin = jnp.int32(0)
    length = jnp.int32(0)
    for i in range(tok_count):
        begin += jnp.where(i < request, place[2 + i], 0)
        length += jnp.where(i == request, place[2 + i], 0)
    begin -= place[0] * chunk_rows
    low = jnp.clip(begin, 0, chunk_rows)
    high = jnp.clip(begin + length, 0, chunk_rows)
    return low, high


def absorb(state, query, keys, values, valid):
    top, acc = state
    factor = math.log2(math.e) / math.sqrt(HEAD_DIM)
    scores = lax.dot_general(query, keys, (((1,), (1,)), ((), ())), preferred_element_type=F32)
    if valid is not None:
        scores = jnp.where(valid, scores, LOWEST)
    new_top = jnp.maximum(top, jnp.max(scores, axis=1, keepdims=True))
    weights = jnp.exp2((scores - new_top) * factor).astype(BF16)
    wide = jnp.concatenate([values, jnp.ones_like(values)], axis=1)
    acc = acc * jnp.exp2((top - new_top) * factor) + jnp.dot(weights, wide, preferred_element_type=F32)
    return new_top, acc


def cached_states(place, request, query, keys, values, tok_count):
    rows, width = query.shape
    chunk_rows = keys.shape[0]
    heads = width // HEAD_DIM
    span = min(512, chunk_rows)
    low, high = key_range(place, request, chunk_rows, tok_count)
    first = low // span
    last = jnp.where(high > low, (high + span - 1) // span, first)

    def step(block, states):
        start = pl.multiple_of(block * span, span)
        spots = start + lax.broadcasted_iota(jnp.int32, (rows, span), 1)
        valid = (spots >= low) & (spots < high)
        out = []
        for j in range(heads):
            cols = slice(j * HEAD_DIM, (j + 1) * HEAD_DIM)
            out.append(
                absorb(states[j], query[:, cols], keys[pl.ds(start, span), cols], values[pl.ds(start, span), cols], valid)
            )
        return tuple(out)

    empty = (jnp.full((rows, 1), LOWEST, F32), jnp.zeros((rows, 2 * HEAD_DIM), F32))
    return lax.fori_loop(first, last, step, (empty,) * heads)


def settle(state):
    top, acc = state
    total = acc[:, HEAD_DIM:]
    some = total > 0.0
    safe = jnp.where(some, total, 1.0)
    log_sum = jnp.where(some, top * (1.0 / math.sqrt(HEAD_DIM)) + jnp.log(safe), LOWEST)
    return acc[:, :HEAD_DIM] / safe, log_sum


def own_kernel(tok_count, place, query, new_keys, new_values, keys, values, mixed_out, log_out):
    states = cached_states(place, place[0], query, keys, values, tok_count)
    for j, state in enumerate(states):
        cols = slice(j * HEAD_DIM, (j + 1) * HEAD_DIM)
        state = absorb(state, query[:, cols], new_keys[:, cols], new_values[:, cols], None)
        mixed, log_sum = settle(state)
        mixed_out[:, cols] = mixed
        log_out[:, cols] = log_sum


def own_part(tok_count, place, query, new_keys, new_values, keys, values):
    rows, width = query.shape
    shape = jax.ShapeDtypeStruct((rows, width), F32)
    return pl.pallas_call(
        functools.partial(own_kernel, tok_count),
        out_shape=(shape, shape),
        in_specs=[SMEM] + [VMEM] * 5,
        out_specs=(VMEM, VMEM),
        compiler_params=params(),
        cost_estimate=cost(4 * rows * width * keys.shape[0], 4 * keys.shape[0] * width),
        name="own_part",
    )(place, query, new_keys, new_values, keys, values)


def away_kernel(tok_count, masks, place, *refs):
    queries, (keys, values), outs = refs[: len(masks)], refs[len(masks) : len(masks) + 2], refs[len(masks) + 2 :]
    for mask, query, out in zip(masks, queries, outs, strict=True):
        rows, width = query.shape
        heads = width // HEAD_DIM
        request = jnp.bitwise_xor(place[0], mask)
        states = cached_states(place, request, query, keys, values, tok_count)
        pieces = []
        for j, state in enumerate(states):
            mixed, log_sum = settle(state)
            out[:rows, j * HEAD_DIM : (j + 1) * HEAD_DIM] = mixed.astype(BF16)
            rest = jnp.transpose(log_sum)[:1, :]
            for _ in range(3):
                piece = rest.astype(BF16).astype(F32)
                pieces.append(piece)
                rest = rest - piece
        at = lax.broadcasted_iota(jnp.int32, (16, rows), 0)
        tail = jnp.zeros((16, rows), F32)
        for i, piece in enumerate(pieces):
            tail = jnp.where(at == i, piece, tail)
        out[rows:, :] = tail.astype(BF16)


def away_parts(tok_count, masks, place, queries, keys, values):
    rows, width = queries[0].shape
    message = jax.ShapeDtypeStruct((rows + 16, width), BF16)
    return pl.pallas_call(
        functools.partial(away_kernel, tok_count, masks),
        out_shape=(message,) * len(masks),
        in_specs=[SMEM] + [VMEM] * (len(masks) + 2),
        out_specs=(VMEM,) * len(masks),
        compiler_params=params(),
        cost_estimate=cost(4 * rows * width * keys.shape[0], 4 * keys.shape[0] * width),
        name="away_parts",
    )(place, *queries, keys, values)


def combine_kernel(share, place, mixed, logs, *refs):
    *messages, keep_out, send_out, whole = refs
    rows, width = mixed.shape
    tails = [message[rows:, :].astype(F32) for message in messages]
    for j in range(width // HEAD_DIM):
        cols = slice(j * HEAD_DIM, (j + 1) * HEAD_DIM)
        parts = [(mixed[:, cols], logs[:, cols])]
        for message, tail in zip(messages, tails, strict=True):
            row = tail[3 * j : 3 * j + 1] + tail[3 * j + 1 : 3 * j + 2] + tail[3 * j + 2 : 3 * j + 3]
            log_sum = jnp.transpose(jnp.broadcast_to(row, (HEAD_DIM, rows)))
            parts.append((message[:rows, cols].astype(F32), log_sum))
        top = functools.reduce(jnp.maximum, [log_sum for _, log_sum in parts])
        total, acc = 0.0, 0.0
        for part, log_sum in parts:
            weight = jnp.exp(log_sum - top)
            total += weight
            acc += weight * part
        whole[:, cols] = (acc / total).astype(BF16)
    head = place[1]
    core = jnp.bitwise_and(head, 1)
    for slot in range(keep_out.shape[0] // share):
        pair = jnp.bitwise_xor(head, 2 * slot) - core
        at = pl.multiple_of((pair + core) * share, share)
        other = pl.multiple_of((pair + 1 - core) * share, share)
        keep_out[slot * share : (slot + 1) * share, :] = whole[pl.ds(at, share), :]
        send_out[slot * share : (slot + 1) * share, :] = whole[pl.ds(other, share), :]


def combine(share, place, mixed, logs, messages):
    rows, width = mixed.shape
    half = jax.ShapeDtypeStruct((rows // 2, width), BF16)
    return pl.pallas_call(
        functools.partial(combine_kernel, share),
        out_shape=(half, half),
        in_specs=[SMEM] + [VMEM] * (len(messages) + 2),
        out_specs=(VMEM, VMEM),
        scratch_shapes=[pltpu.VMEM((rows, width), BF16)],
        compiler_params=params(),
        cost_estimate=cost(rows * width * 40, rows * width * 16),
        name="combine",
    )(place, mixed, logs, *messages)


def out_kernel(keep, other, w_keep, w_other, *outs):
    share = outs[0].shape[0]
    total = jnp.dot(keep[...], w_keep[...], preferred_element_type=F32)
    total += jnp.dot(other[...], w_other[...], preferred_element_type=F32)
    for slot, out in enumerate(outs):
        out[...] = total[slot * share : (slot + 1) * share].astype(out.dtype)


def out_project(share, keep, other, w_keep, w_other):
    half, width = keep.shape
    full = w_keep.shape[1]
    return pl.pallas_call(
        out_kernel,
        out_shape=tuple(jax.ShapeDtypeStruct((share, full), F32 if s == 0 else BF16) for s in range(half // share)),
        in_specs=[VMEM] * 4,
        out_specs=(VMEM,) * (half // share),
        compiler_params=params(),
        cost_estimate=cost(4 * half * width * full, 4 * width * full),
        name="out_project",
    )(keep, other, w_keep, w_other)


def finish_kernel(last, own, *refs):
    *others, residual, attn_gain, final_gain, first_out = refs[: len(refs) - (0 if last else 2)]
    total = own[...]
    for other in others:
        total += other[...].astype(F32)
    scale = lax.rsqrt(jnp.mean(total * total, axis=1, keepdims=True) + EPSILON)
    first = (residual[...].astype(F32) + total * scale * attn_gain[...]).astype(BF16)
    first_out[...] = first
    if not last:
        normed_out, square_out = refs[-2:]
        wide = first.astype(F32)
        squares = jnp.sum(wide * wide, axis=1, keepdims=True)
        scale = lax.rsqrt(squares / wide.shape[1] + EPSILON)
        normed_out[...] = (wide * scale * final_gain[...]).astype(BF16)
        square_out[...] = jnp.broadcast_to(jnp.sum(squares, axis=0, keepdims=True), square_out.shape)


def finish(last, own, others, residual, attn_gain, final_gain):
    state = jax.ShapeDtypeStruct(residual.shape, BF16)
    outs = (state,) if last else (state, state, jax.ShapeDtypeStruct((1, 128), F32))
    return pl.pallas_call(
        functools.partial(finish_kernel, last),
        out_shape=outs,
        in_specs=[VMEM] * (len(others) + 4),
        out_specs=(VMEM,) * len(outs),
        compiler_params=params(),
        cost_estimate=cost(residual.size * 20, residual.size * 12),
        name="finish",
    )(own, *others, residual, attn_gain, final_gain)


def logits_kernel(share, tok_count, place, mine, other, lm_block, best_out, x):
    @pl.when(pl.program_id(0) == 0)
    def _():
        core = jnp.bitwise_and(place[1], 1)
        for flag, piece in enumerate((mine, other)):
            for slot in range(tok_count):
                tok = jnp.bitwise_xor(place[0], slot)
                at = pl.multiple_of((2 * tok + jnp.bitwise_xor(core, flag)) * share, share)
                x[pl.ds(at, share), :] = piece[slot * share : (slot + 1) * share, :]
        best_out[...] = jnp.full(best_out.shape, -jnp.inf, F32)

    logits = lax.dot_general(lm_block[...], x[...], (((1,), (1,)), ((), ())), preferred_element_type=F32)
    best = jnp.max(logits.reshape(logits.shape[0] // 8, 8, logits.shape[1]), axis=0)
    best_out[...] = jnp.maximum(best_out[...], best)


def largest_logits(share, tok_count, place, mine, other, lm_head):
    half, full = mine.shape
    vocab = lm_head.shape[0]
    span = vocab // 7
    return pl.pallas_call(
        functools.partial(logits_kernel, share, tok_count),
        out_shape=jax.ShapeDtypeStruct((8, 2 * half), F32),
        grid=(vocab // span,),
        in_specs=[SMEM, VMEM, VMEM, pl.BlockSpec((span, full), lambda i: (i, 0))],
        out_specs=VMEM,
        scratch_shapes=[pltpu.VMEM((2 * half, full), BF16)],
        compiler_params=params(),
        cost_estimate=cost(4 * half * full * vocab, 2 * full * vocab),
        name="largest_logits",
    )(place, mine, other, lm_head)


def gather_best_kernel(place, square, *refs):
    *bests, out = refs
    chip = place[1] // 2
    out[...] = jnp.zeros(out.shape, F32)
    for slot, best in enumerate(bests):
        out[pl.ds(jnp.bitwise_xor(chip, slot), 1), :] = jnp.max(best[...], axis=0, keepdims=True)
    lanes = lax.broadcasted_iota(jnp.int32, (1, out.shape[1]), 1)
    out[len(bests) : len(bests) + 1, :] = jnp.where(lanes == place[0], square[:, :1], 0.0)


def gather_best(place, square, bests):
    rows = -(-(len(bests) + 1) // 8) * 8
    return pl.pallas_call(
        gather_best_kernel,
        out_shape=jax.ShapeDtypeStruct((rows, bests[0].shape[1]), F32),
        in_specs=[SMEM] + [VMEM] * (1 + len(bests)),
        out_specs=VMEM,
        compiler_params=params(),
        name="gather_best",
    )(place, square, *bests)


def shards(
    block_states,
    token_ids,
    accept,
    cache_lengths,
    cache_keys,
    cache_values,
    w_query,
    w_key,
    w_value,
    w_out,
    attn_gain,
    final_gain,
    embed,
    lm_head,
):
    tok_index = lax.axis_index("tok")
    head_index = lax.axis_index("head")
    tok_count = lax.axis_size("tok")
    head_count = lax.axis_size("head")
    chips = head_count // 2
    block_rows = block_states.shape[0]
    share = block_rows // head_count
    model_width = w_query.shape[0]
    place = jnp.concatenate([jnp.stack([tok_index, head_index]).astype(jnp.int32), cache_lengths])
    gains = (attn_gain.reshape(1, -1), final_gain.reshape(1, -1))
    tok_masks = range(1, tok_count)

    def by_head(value, mask):
        return lax.ppermute(value, "head", xor_pairs(head_count, mask))

    def by_tok(value, mask):
        return lax.ppermute(value, "tok", xor_pairs(tok_count, mask))

    def run_layer(features, last):
        chip_pieces = [features] + [by_head(features, 2 * s) for s in range(1, chips)]
        core_pieces = [by_head(piece, 1) for piece in chip_pieces]
        pieces = [piece for pair in zip(chip_pieces, core_pieces, strict=True) for piece in pair]
        query, key, value, residual = project(place, pieces, w_query, w_key, w_value)
        queries = [by_tok(query, mask) for mask in tok_masks]
        mixed, logs = own_part(tok_count, place, query, key, value, cache_keys, cache_values)
        messages = away_parts(tok_count, tok_masks, place, queries, cache_keys, cache_values)
        messages = [by_tok(message, mask) for mask, message in zip(tok_masks, messages, strict=True)]
        keep, send = combine(share, place, mixed, logs, messages)
        own, *sums = out_project(share, keep, by_head(send, 1), w_out, w_out_other)
        sums = [by_head(total, 2 * s) for s, total in enumerate(sums, 1)]
        return finish(last, own, sums, residual, *gains)

    w_out_other = by_head(w_out, 1)

    _, normed, square = run_layer(block_states, False)

    vocab_here = embed.shape[0]
    local_ids = jnp.clip(token_ids - tok_index * vocab_here, 0, vocab_here - 1).reshape(tok_count, block_rows)
    owners = lax.dynamic_slice_in_dim(token_ids, tok_index * block_rows, block_rows, 0) // vocab_here
    chosen = block_states
    for mask in range(tok_count):
        other = jnp.bitwise_xor(tok_index, mask)
        ids = lax.dynamic_slice_in_dim(local_ids, other, 1, 0)[0]
        found = jnp.take(embed, ids, axis=0, mode="clip")
        if mask:
            found = by_tok(found, mask)
        chosen = jnp.where(((accept == 1) & (owners == other))[:, None], found, chosen)
    (hiddens,) = run_layer(chosen, True)

    column = jnp.concatenate([normed] + [by_tok(normed, mask) for mask in tok_masks], axis=0)
    if chips == 4:
        along_x, along_y = by_head(column, 2), by_head(column, 4)
        half = column.shape[0] // 2
        across = jnp.concatenate([by_head(along_y[:half], 2), by_head(along_x[half:], 4)], axis=0)
        columns = [column, along_x, along_y, across]
    else:
        columns = [column] + [by_head(column, 2 * s) for s in range(1, chips)]
    bests = [largest_logits(share, tok_count, place, piece, by_head(piece, 1), lm_head) for piece in columns]
    best = gather_best(place, square, bests)
    is_max = lax.broadcasted_iota(jnp.int32, best.shape, 0) < chips
    for axis, size in (("head", head_count), ("tok", tok_count)):
        mask = 1
        while mask < size:
            other = lax.ppermute(best, axis, xor_pairs(size, mask))
            best = jnp.where(is_max, jnp.maximum(best, other), best + other)
            mask *= 2
    top_logits = best[:chips].reshape(chips, tok_count, 2, share).transpose(1, 0, 2, 3).reshape(-1)
    request_norms = jnp.sqrt(best[chips, :tok_count] / (block_rows * model_width))
    return (hiddens, request_norms, top_logits)


def solution(mesh):
    placed = (
        P("tok", "head"),
        P(),
        P("tok"),
        P(),
        P("tok", "head"),
        P("tok", "head"),
        P(None, "head"),
        P(None, "head"),
        P(None, "head"),
        P("head", None),
        P(),
        P(),
        P("tok", "head"),
        P(("tok", "head"), None),
    )
    return jax.shard_map(
        shards,
        mesh=mesh,
        in_specs=placed,
        out_specs=(P(("tok", "head"), None), P(), P()),
        check_vma=False,
    )
```

```python
import functools
import math

import jax
import jax.numpy as jnp
from jax import lax
from jax.experimental import pallas as pl
from jax.experimental.pallas import tpu as pltpu
from jax.sharding import PartitionSpec as P

HEAD_DIM = 128
EPSILON = 1e-06
LOWEST = -1e30
BF16 = jnp.bfloat16
F32 = jnp.float32

SMEM = pl.BlockSpec(memory_space=pltpu.SMEM)
VMEM = pl.BlockSpec(memory_space=pltpu.VMEM)
HBM = pl.BlockSpec(memory_space=pltpu.HBM)


def params(mib=24):
    return pltpu.CompilerParams(vmem_limit_bytes=mib * 2**20)


def cost(flops, moved):
    return pl.CostEstimate(flops=flops, bytes_accessed=moved, transcendentals=0)


def call(kernel, operands, after=(), in_specs=None, **rest):
    count = len(operands)

    def body(*refs):
        kernel(*refs[:count], *refs[count + len(after) :])

    specs = list(in_specs) + [pl.BlockSpec(memory_space=pl.ANY)] * len(after)
    return pl.pallas_call(body, in_specs=specs, **rest)(*operands, *after)


def xor_pairs(size, mask):
    return [(i, i ^ mask) for i in range(size)]


def fetch(sources, targets, sems):
    copies = [pltpu.make_async_copy(a, b, sems.at[i]) for i, (a, b) in enumerate(zip(sources, targets, strict=True))]
    for copy in copies:
        copy.start()
    return copies


def project_kernel(place, *refs):
    *pieces, wq, wk, wv, q_out, k_out, v_out, res_out, x = refs
    head = place[1]
    rows, width = q_out.shape
    for odd in range(2):
        mask = odd
        for piece in pieces[odd * len(pieces) // 2 : (odd + 1) * len(pieces) // 2]:
            for start in range(0, piece.shape[0], rows):
                at = pl.multiple_of(jnp.bitwise_xor(head, mask) * width, width)
                x[:, pl.ds(at, width)] = piece[start : start + rows, :]
                mask += 2
    for w, out in ((wq, q_out), (wk, k_out), (wv, v_out)):
        out[...] = jnp.dot(x[...], w[...], preferred_element_type=F32).astype(BF16)
    share = res_out.shape[0]
    res_out[...] = x[pl.ds(pl.multiple_of(head * share, share), share), :]


def project(rows, place, pieces, wq, wk, wv, after=()):
    full, width = wq.shape
    share = rows // (full // width)
    tile = jax.ShapeDtypeStruct((rows, width), BF16)
    return call(
        project_kernel,
        (place, *pieces, wq, wk, wv),
        after,
        out_shape=(tile, tile, tile, jax.ShapeDtypeStruct((share, full), BF16)),
        in_specs=[SMEM] + [VMEM] * (len(pieces) + 3),
        out_specs=(VMEM,) * 4,
        scratch_shapes=[pltpu.VMEM((rows, full), BF16)],
        compiler_params=params(),
        cost_estimate=cost(6 * rows * full * width, 8 * full * width),
        name="project",
    )


def key_range(place, request, chunk, chunk_rows, tok_count):
    begin = jnp.int32(0)
    length = jnp.int32(0)
    for i in range(tok_count):
        begin += jnp.where(i < request, place[2 + i], 0)
        length += jnp.where(i == request, place[2 + i], 0)
    begin -= chunk * chunk_rows
    low = jnp.clip(begin, 0, chunk_rows)
    high = jnp.clip(begin + length, 0, chunk_rows)
    return low, high


def absorb(state, query, keys, values, valid):
    top, acc = state
    factor = math.log2(math.e) / math.sqrt(HEAD_DIM)
    scores = lax.dot_general(query, keys, (((1,), (1,)), ((), ())), preferred_element_type=F32)
    if valid is not None:
        scores = jnp.where(valid, scores, LOWEST)
    new_top = jnp.maximum(top, jnp.max(scores, axis=1, keepdims=True))
    weights = jnp.exp2((scores - new_top) * factor).astype(BF16)
    wide = jnp.concatenate([values, jnp.ones_like(values)], axis=1)
    acc = acc * jnp.exp2((top - new_top) * factor) + jnp.dot(weights, wide, preferred_element_type=F32)
    return new_top, acc


def cached_states(place, request, query, keys, values, tok_count):
    rows, width = query.shape
    chunk_rows = keys.shape[0]
    heads = width // HEAD_DIM
    span = min(512, chunk_rows)
    low, high = key_range(place, request, place[0], chunk_rows, tok_count)
    first = low // span
    last = jnp.where(high > low, (high + span - 1) // span, first)

    def step(block, states):
        start = pl.multiple_of(block * span, span)
        spots = start + lax.broadcasted_iota(jnp.int32, (rows, span), 1)
        valid = (spots >= low) & (spots < high)
        out = []
        for j in range(heads):
            cols = slice(j * HEAD_DIM, (j + 1) * HEAD_DIM)
            out.append(
                absorb(states[j], query[:, cols], keys[pl.ds(start, span), cols], values[pl.ds(start, span), cols], valid)
            )
        return tuple(out)

    empty = (jnp.full((rows, 1), LOWEST, F32), jnp.zeros((rows, 2 * HEAD_DIM), F32))
    return lax.fori_loop(first, last, step, (empty,) * heads)


def settle(state):
    top, acc = state
    total = acc[:, HEAD_DIM:]
    some = total > 0.0
    safe = jnp.where(some, total, 1.0)
    log_sum = jnp.where(some, top * (1.0 / math.sqrt(HEAD_DIM)) + jnp.log(safe), LOWEST)
    return acc[:, :HEAD_DIM] / safe, log_sum


def own_kernel(tok_count, place, query, new_keys, new_values, keys, values, mixed_out, log_out):
    states = cached_states(place, place[0], query, keys, values, tok_count)
    for j, state in enumerate(states):
        cols = slice(j * HEAD_DIM, (j + 1) * HEAD_DIM)
        state = absorb(state, query[:, cols], new_keys[:, cols], new_values[:, cols], None)
        mixed, log_sum = settle(state)
        mixed_out[:, cols] = mixed
        log_out[:, cols] = log_sum


def own_part(tok_count, place, query, new_keys, new_values, keys, values, after=()):
    rows, width = query.shape
    shape = jax.ShapeDtypeStruct((rows, width), F32)
    return call(
        functools.partial(own_kernel, tok_count),
        (place, query, new_keys, new_values, keys, values),
        after,
        out_shape=(shape, shape),
        in_specs=[SMEM] + [VMEM] * 5,
        out_specs=(VMEM, VMEM),
        compiler_params=params(),
        cost_estimate=cost(4 * rows * width * keys.shape[0], 4 * keys.shape[0] * width),
        name="own_part",
    )


def away_part(place, mask, query, keys, values, out, tok_count):
    rows, width = query.shape
    states = cached_states(place, jnp.bitwise_xor(place[0], mask), query, keys, values, tok_count)
    pieces = []
    for j, state in enumerate(states):
        mixed, log_sum = settle(state)
        out[:rows, j * HEAD_DIM : (j + 1) * HEAD_DIM] = mixed.astype(BF16)
        rest = jnp.transpose(log_sum)[:1, :]
        for _ in range(3):
            piece = rest.astype(BF16).astype(F32)
            pieces.append(piece)
            rest = rest - piece
    at = lax.broadcasted_iota(jnp.int32, (16, rows), 0)
    tail = jnp.zeros((16, rows), F32)
    for i, piece in enumerate(pieces):
        tail = jnp.where(at == i, piece, tail)
    out[rows : rows + 16, :] = tail.astype(BF16)


def second_kernel(tok_count, masks, place, *refs):
    count = len(masks)
    queries, (keys, values), refs = refs[:count], refs[count : count + 2], refs[count + 2 :]
    messages, x = refs[-5 - count : -5], refs[-1]
    project_kernel(place, *refs[: -5 - count], *refs[-5:-1], x)
    new_query = refs[-5]
    rows = new_query.shape[0]
    for mask, query, message in zip(masks, queries, messages, strict=True):
        away_part(place, mask, query, keys, values, message, tok_count)
        message[rows + 16 :, :] = new_query[...]


def second_stage(tok_count, masks, place, queries, keys, values, pieces, wq, wk, wv, after=()):
    rows, width = queries[0].shape
    full = wq.shape[0]
    share = rows // (full // width)
    tile = jax.ShapeDtypeStruct((rows, width), BF16)
    message = jax.ShapeDtypeStruct((2 * rows + 16, width), BF16)
    outs = (message,) * len(masks) + (tile, tile, tile, jax.ShapeDtypeStruct((share, full), BF16))
    results = call(
        functools.partial(second_kernel, tok_count, masks),
        (place, *queries, keys, values, *pieces, wq, wk, wv),
        after,
        out_shape=outs,
        in_specs=[SMEM] + [VMEM] * (len(masks) + len(pieces) + 5),
        out_specs=(VMEM,) * len(outs),
        scratch_shapes=[pltpu.VMEM((rows, full), BF16)],
        compiler_params=params(),
        cost_estimate=cost(4 * rows * width * keys.shape[0] + 6 * rows * full * width, 8 * full * width),
        name="second_stage",
    )
    return results[: len(masks)], results[len(masks) :]


def third_kernel(share, tok_count, masks, place, mixed, logs, *refs):
    count = len(masks)
    messages, (keys, values), (keep, send), outs, whole = (
        refs[:count],
        refs[count : count + 2],
        refs[count + 2 : count + 4],
        refs[count + 4 : -1],
        refs[-1],
    )
    combine_kernel(share, place, mixed, logs, *messages, keep, send, whole)
    rows = mixed.shape[0]
    for mask, message, out in zip(masks, messages, outs, strict=True):
        away_part(place, mask, message.at[pl.ds(rows + 16, rows), :], keys, values, out, tok_count)


def third_stage(share, tok_count, masks, place, mixed, logs, messages, keys, values, after=()):
    rows, width = mixed.shape
    half = jax.ShapeDtypeStruct((rows // 2, width), BF16)
    message = jax.ShapeDtypeStruct((rows + 16, width), BF16)
    results = call(
        functools.partial(third_kernel, share, tok_count, masks),
        (place, mixed, logs, *messages, keys, values),
        after,
        out_shape=(half, half) + (message,) * len(masks),
        in_specs=[SMEM] + [VMEM] * (4 + len(masks)),
        out_specs=(VMEM,) * (2 + len(masks)),
        scratch_shapes=[pltpu.VMEM((rows, width), BF16)],
        compiler_params=params(),
        cost_estimate=cost(4 * rows * width * keys.shape[0], 4 * keys.shape[0] * width),
        name="third_stage",
    )
    return results[:2], results[2:]


def combine_kernel(share, place, mixed, logs, *refs):
    *messages, keep_out, send_out, whole = refs
    rows, width = mixed.shape
    tails = [message[rows : rows + 16, :].astype(F32) for message in messages]
    for j in range(width // HEAD_DIM):
        cols = slice(j * HEAD_DIM, (j + 1) * HEAD_DIM)
        parts = [(mixed[:, cols], logs[:, cols])]
        for message, tail in zip(messages, tails, strict=True):
            row = tail[3 * j : 3 * j + 1] + tail[3 * j + 1 : 3 * j + 2] + tail[3 * j + 2 : 3 * j + 3]
            log_sum = jnp.transpose(jnp.broadcast_to(row, (HEAD_DIM, rows)))
            parts.append((message[:rows, cols].astype(F32), log_sum))
        top = functools.reduce(jnp.maximum, [log_sum for _, log_sum in parts])
        total, acc = 0.0, 0.0
        for part, log_sum in parts:
            weight = jnp.exp(log_sum - top)
            total += weight
            acc += weight * part
        whole[:, cols] = (acc / total).astype(BF16)
    head = place[1]
    core = jnp.bitwise_and(head, 1)
    for slot in range(keep_out.shape[0] // share):
        pair = jnp.bitwise_xor(head, 2 * slot) - core
        at = pl.multiple_of((pair + core) * share, share)
        other = pl.multiple_of((pair + 1 - core) * share, share)
        keep_out[slot * share : (slot + 1) * share, :] = whole[pl.ds(at, share), :]
        send_out[slot * share : (slot + 1) * share, :] = whole[pl.ds(other, share), :]


def combine(share, place, mixed, logs, messages, after=()):
    rows, width = mixed.shape
    half = jax.ShapeDtypeStruct((rows // 2, width), BF16)
    return call(
        functools.partial(combine_kernel, share),
        (place, mixed, logs, *messages),
        after,
        out_shape=(half, half),
        in_specs=[SMEM] + [VMEM] * (len(messages) + 2),
        out_specs=(VMEM, VMEM),
        scratch_shapes=[pltpu.VMEM((rows, width), BF16)],
        compiler_params=params(),
        cost_estimate=cost(rows * width * 40, rows * width * 16),
        name="combine",
    )


def ids_kernel(vocab_here, place, ids, local_out, owner_out):
    for slot in range(ids.shape[0]):
        row = ids[pl.ds(jnp.bitwise_xor(place[0], slot), 1), :]
        local_out[slot : slot + 1, :] = jnp.clip(row - place[0] * vocab_here, 0, vocab_here - 1)
        if slot == 0:
            owner = jnp.zeros(row.shape, jnp.int32)
            for i in range(1, ids.shape[0]):
                owner += jnp.where(row >= i * vocab_here, 1, 0)
            owner_out[...] = owner


def sort_ids(vocab_here, place, ids, after=()):
    return call(
        functools.partial(ids_kernel, vocab_here),
        (place, ids),
        after,
        out_shape=(
            jax.ShapeDtypeStruct(ids.shape, jnp.int32),
            jax.ShapeDtypeStruct((1, ids.shape[1]), jnp.int32),
        ),
        in_specs=[SMEM, VMEM],
        out_specs=(VMEM, VMEM),
        compiler_params=params(),
        name="sort_ids",
    )


def choose_kernel(place, accept, owner, states, *refs):
    *found, out = refs
    rows = states.shape[0]
    slot = jnp.where(accept[...] == 1, jnp.bitwise_xor(owner[...], place[0]), len(found)).astype(F32)
    slot = jnp.transpose(jnp.broadcast_to(slot, (128, rows)))
    for start in range(0, states.shape[1], 128):
        cols = slice(start, start + 128)
        value = states[:, cols].astype(F32)
        for i, rows_found in enumerate(found):
            value = jnp.where(slot == i, rows_found[:, cols].astype(F32), value)
        out[:, cols] = value.astype(BF16)


def choose(place, accept, owner, states, found, after=()):
    return call(
        choose_kernel,
        (place, accept, owner, states, *found),
        after,
        out_shape=jax.ShapeDtypeStruct(states.shape, BF16),
        in_specs=[SMEM] + [VMEM] * (3 + len(found)),
        out_specs=VMEM,
        compiler_params=params(),
        name="choose",
    )


def stack_kernel(*refs):
    *pieces, out = refs
    at = 0
    for piece in pieces:
        out[at : at + piece.shape[0], :] = piece[...]
        at += piece.shape[0]


def stack(pieces, after=()):
    rows = sum(piece.shape[0] for piece in pieces)
    return call(
        stack_kernel,
        tuple(pieces),
        after,
        out_shape=jax.ShapeDtypeStruct((rows, pieces[0].shape[1]), BF16),
        in_specs=[VMEM] * len(pieces),
        out_specs=VMEM,
        compiler_params=params(),
        name="stack",
    )


def out_kernel(keep, other, w_keep, w_other, *outs):
    share = outs[0].shape[0]
    total = jnp.dot(other[...], w_other[...], preferred_element_type=F32)
    total += jnp.dot(keep[...], w_keep[...], preferred_element_type=F32)
    for slot, out in enumerate(outs):
        out[...] = total[slot * share : (slot + 1) * share].astype(out.dtype)


def out_project(share, keep, other, w_keep, w_other):
    half, width = keep.shape
    full = w_keep.shape[1]
    return pl.pallas_call(
        out_kernel,
        out_shape=tuple(jax.ShapeDtypeStruct((share, full), F32 if s == 0 else BF16) for s in range(half // share)),
        in_specs=[VMEM] * 4,
        out_specs=(VMEM,) * (half // share),
        compiler_params=params(),
        cost_estimate=cost(4 * half * width * full, 4 * width * full),
        name="out_project",
    )(keep, other, w_keep, w_other)


def finish_kernel(last, own, *refs):
    *refs, attn_gain, final_gain, sems = refs
    *others, residual, attn_far, final_far, first_out = refs[: len(refs) - (0 if last else 2)]
    copies = fetch((attn_far, final_far), (attn_gain, final_gain), sems)
    total = own[...]
    for other in others:
        total += other[...].astype(F32)
    scale = lax.rsqrt(jnp.mean(total * total, axis=1, keepdims=True) + EPSILON)
    for copy in copies:
        copy.wait()
    first = (residual[...].astype(F32) + total * scale * attn_gain[...]).astype(BF16)
    first_out[...] = first
    if not last:
        normed_out, square_out = refs[-2:]
        wide = first.astype(F32)
        squares = jnp.sum(wide * wide, axis=1, keepdims=True)
        scale = lax.rsqrt(squares / wide.shape[1] + EPSILON)
        normed_out[...] = (wide * scale * final_gain[...]).astype(BF16)
        square_out[...] = jnp.broadcast_to(jnp.sum(squares, axis=0, keepdims=True), square_out.shape)


def finish(last, own, others, residual, attn_gain, final_gain, after=()):
    state = jax.ShapeDtypeStruct(residual.shape, BF16)
    outs = (state,) if last else (state, state, jax.ShapeDtypeStruct((1, 128), F32))
    return call(
        functools.partial(finish_kernel, last),
        (own, *others, residual, attn_gain, final_gain),
        after,
        out_shape=outs,
        in_specs=[VMEM] * (len(others) + 2) + [HBM] * 2,
        out_specs=(VMEM,) * len(outs),
        scratch_shapes=[pltpu.VMEM(attn_gain.shape, F32)] * 2 + [pltpu.SemaphoreType.DMA((2,))],
        compiler_params=params(),
        cost_estimate=cost(residual.size * 20, residual.size * 12),
        name="finish",
    )


def logits_kernel(share, tok_count, place, mine, other, lm_block, best_out, x):
    @pl.when(pl.program_id(0) == 0)
    def _():
        core = jnp.bitwise_and(place[1], 1)
        for flag, piece in enumerate((mine, other)):
            for slot in range(tok_count):
                tok = jnp.bitwise_xor(place[0], slot)
                at = pl.multiple_of((2 * tok + jnp.bitwise_xor(core, flag)) * share, share)
                x[pl.ds(at, share), :] = piece[slot * share : (slot + 1) * share, :]
        best_out[...] = jnp.full(best_out.shape, -jnp.inf, F32)

    logits = lax.dot_general(lm_block[...], x[...], (((1,), (1,)), ((), ())), preferred_element_type=F32)
    best = jnp.max(logits.reshape(logits.shape[0] // 8, 8, logits.shape[1]), axis=0)
    best_out[...] = jnp.maximum(best_out[...], best)


def largest_logits(share, tok_count, place, mine, other, lm_head, after=()):
    half, full = mine.shape
    vocab = lm_head.shape[0]
    span = vocab // 4 if vocab % 64 == 0 else vocab // 7
    return call(
        functools.partial(logits_kernel, share, tok_count),
        (place, mine, other, lm_head),
        after,
        out_shape=jax.ShapeDtypeStruct((8, 2 * half), F32),
        grid=(vocab // span,),
        in_specs=[SMEM, VMEM, VMEM, pl.BlockSpec((span, full), lambda i: (i, 0))],
        out_specs=VMEM,
        scratch_shapes=[pltpu.VMEM((2 * half, full), BF16)],
        compiler_params=params(),
        cost_estimate=cost(4 * half * full * vocab, 2 * full * vocab),
        name="largest_logits",
    )


def gather_best_kernel(place, square, *refs):
    *bests, out = refs
    chip = place[1] // 2
    out[...] = jnp.zeros(out.shape, F32)
    for slot, best in enumerate(bests):
        out[pl.ds(jnp.bitwise_xor(chip, slot), 1), :] = jnp.max(best[...], axis=0, keepdims=True)
    lanes = lax.broadcasted_iota(jnp.int32, (1, out.shape[1]), 1)
    out[len(bests) : len(bests) + 1, :] = jnp.where(lanes == place[0], square[:, :1], 0.0)


def gather_best(place, square, bests):
    rows = -(-(len(bests) + 1) // 8) * 8
    return pl.pallas_call(
        gather_best_kernel,
        out_shape=jax.ShapeDtypeStruct((rows, bests[0].shape[1]), F32),
        in_specs=[SMEM] + [VMEM] * (1 + len(bests)),
        out_specs=VMEM,
        compiler_params=params(),
        name="gather_best",
    )(place, square, *bests)


def shards(
    block_states,
    token_ids,
    accept,
    cache_lengths,
    cache_keys,
    cache_values,
    w_query,
    w_key,
    w_value,
    w_out,
    attn_gain,
    final_gain,
    embed,
    lm_head,
):
    tok_index = lax.axis_index("tok")
    head_index = lax.axis_index("head")
    tok_count = lax.axis_size("tok")
    head_count = lax.axis_size("head")
    chips = head_count // 2
    block_rows = block_states.shape[0]
    share = block_rows // head_count
    model_width = w_query.shape[0]
    place = jnp.concatenate([jnp.stack([tok_index, head_index]).astype(jnp.int32), cache_lengths])
    gains = (attn_gain.reshape(1, -1), final_gain.reshape(1, -1))
    tok_masks = range(1, tok_count)

    def by_head(value, mask):
        return lax.ppermute(value, "head", xor_pairs(head_count, mask))

    def by_tok(value, mask):
        return lax.ppermute(value, "tok", xor_pairs(tok_count, mask))

    def spread(features):
        pieces = [features] + [by_head(features, 2 * s) for s in range(1, chips)]
        return pieces, [by_head(piece, 1) for piece in pieces]

    def exchange(arrays):
        return [by_tok(array, mask) for mask, array in zip(tok_masks, arrays, strict=True)]

    def own_of(query, key, value, after=()):
        return own_part(tok_count, place, query, key, value, cache_keys, cache_values, after)

    def join(own, messages, after=()):
        return combine(share, place, *own, messages, after)

    def out_layer(keep, send):
        return out_project(share, keep, by_head(send, 1), w_out, w_out_other)

    def finish_layer(last, sums, residual, after=()):
        own, *others = sums
        others = [by_head(total, 2 * s) for s, total in enumerate(others, 1)]
        return finish(last, own, others, residual, *gains, after)


    w_out_other = by_head(w_out, 1)

    vocab_here = embed.shape[0]
    ids, owners = sort_ids(vocab_here, place, token_ids.reshape(tok_count, block_rows))
    found = embed.at[ids.reshape(-1)].get(mode="promise_in_bounds").reshape(tok_count, block_rows, -1)
    found = [found[mask] for mask in range(tok_count)]
    embedded = [found[0], *exchange(found[1:])]

    pieces, others = spread(block_states)
    query, key, value, residual = project(
        block_rows, place, pieces + others, w_query, w_key, w_value, [w_out_other, found[1]]
    )
    queries = exchange([query] * len(tok_masks))
    own = own_of(query, key, value)
    chosen = choose(place, accept.reshape(1, -1), owners, block_states, embedded, queries[:1])
    pieces, others = spread(chosen)
    messages, (query, key, value, residual_two) = second_stage(
        tok_count, tok_masks, place, queries, cache_keys, cache_values, pieces + others, w_query, w_key, w_value, [own[0]]
    )
    messages = exchange(messages)
    own_two = own_of(query, key, value)
    keep, messages = third_stage(
        share, tok_count, tok_masks, place, *own, messages, cache_keys, cache_values, [own_two[0]]
    )
    messages = exchange(messages)
    _, normed, square = finish_layer(False, out_layer(*keep), residual)

    column = stack([normed] + exchange([normed] * len(tok_masks)), messages)

    def best_of(piece, after=()):
        return largest_logits(share, tok_count, place, piece, by_head(piece, 1), lm_head, after)

    if chips == 4:
        along_x, along_y = by_head(column, 2), by_head(column, 4)
        half = column.shape[0] // 2
        across = stack([by_head(along_y[:half], 2), by_head(along_x[half:], 4)])
        columns = [column, along_x, along_y, across]
    else:
        columns = [column] + [by_head(column, 2 * s) for s in range(1, chips)]
    bests = []
    for piece in columns:
        bests.append(best_of(piece, bests[-1:]))
    sums = out_layer(*join(own_two, messages))
    (hiddens,) = finish_layer(True, sums, residual_two)

    best = gather_best(place, square, bests)
    is_max = lax.broadcasted_iota(jnp.int32, best.shape, 0) < chips
    for axis, size in (("head", head_count), ("tok", tok_count)):
        mask = 1
        while mask < size:
            other = lax.ppermute(best, axis, xor_pairs(size, mask))
            best = jnp.where(is_max, jnp.maximum(best, other), best + other)
            mask *= 2
    top_logits = best[:chips].reshape(chips, tok_count, 2, share).transpose(1, 0, 2, 3).reshape(-1)
    request_norms = jnp.sqrt(best[chips, :tok_count] / (block_rows * model_width))
    return (hiddens, request_norms, top_logits)


def solution(mesh):
    placed = (
        P("tok", "head"),
        P(),
        P("tok"),
        P(),
        P("tok", "head"),
        P("tok", "head"),
        P(None, "head"),
        P(None, "head"),
        P(None, "head"),
        P("head", None),
        P(),
        P(),
        P("tok", "head"),
        P(("tok", "head"), None),
    )
    return jax.shard_map(
        shards,
        mesh=mesh,
        in_specs=placed,
        out_specs=(P(("tok", "head"), None), P(), P()),
        check_vma=False,
    )
```

```python
import functools
import math

import jax
import jax.numpy as jnp
from jax import lax
from jax.experimental import pallas as pl
from jax.experimental.pallas import tpu as pltpu
from jax.sharding import PartitionSpec as P

HEAD_DIM = 128
EPSILON = 1e-06
LOWEST = -1e30
BF16 = jnp.bfloat16
F32 = jnp.float32

SMEM = pl.BlockSpec(memory_space=pltpu.SMEM)
VMEM = pl.BlockSpec(memory_space=pltpu.VMEM)
HBM = pl.BlockSpec(memory_space=pltpu.HBM)


def params(mib=24):
    return pltpu.CompilerParams(vmem_limit_bytes=mib * 2**20)


def cost(flops, moved):
    return pl.CostEstimate(flops=flops, bytes_accessed=moved, transcendentals=0)


def call(kernel, operands, after=(), in_specs=None, **rest):
    count = len(operands)

    def body(*refs):
        kernel(*refs[:count], *refs[count + len(after) :])

    specs = list(in_specs) + [pl.BlockSpec(memory_space=pl.ANY)] * len(after)
    return pl.pallas_call(body, in_specs=specs, **rest)(*operands, *after)


def xor_pairs(size, mask):
    return [(i, i ^ mask) for i in range(size)]


def fetch(sources, targets, sems):
    copies = [pltpu.make_async_copy(a, b, sems.at[i]) for i, (a, b) in enumerate(zip(sources, targets, strict=True))]
    for copy in copies:
        copy.start()
    return copies


def carry_kernel(*refs):
    count = len(refs) // 2
    for source, out in zip(refs[:count], refs[count:], strict=True):
        out[...] = source[...]


def carry(*arrays):
    return pl.pallas_call(
        carry_kernel,
        out_shape=tuple(jax.ShapeDtypeStruct(a.shape, a.dtype) for a in arrays),
        in_specs=[VMEM] * len(arrays),
        out_specs=(VMEM,) * len(arrays),
        compiler_params=params(),
        name="carry",
    )(*arrays)


def first_kernel(place, *refs):
    project_kernel(place, *refs[:-5], refs[-1])
    for source, out in zip((refs[0], *refs[-12:-9]), refs[-5:-1], strict=True):
        out[...] = source[...]


def project_kernel(place, *refs):
    *pieces, wq, wk, wv, q_out, k_out, v_out, res_out, x = refs
    head = place[1]
    rows, width = q_out.shape
    for odd in range(2):
        mask = odd
        for piece in pieces[odd * len(pieces) // 2 : (odd + 1) * len(pieces) // 2]:
            for start in range(0, piece.shape[0], rows):
                at = pl.multiple_of(jnp.bitwise_xor(head, mask) * width, width)
                x[:, pl.ds(at, width)] = piece[start : start + rows, :]
                mask += 2
    for w, out in ((wq, q_out), (wk, k_out), (wv, v_out)):
        out[...] = jnp.dot(x[...], w[...], preferred_element_type=F32).astype(BF16)
    share = res_out.shape[0]
    res_out[...] = x[pl.ds(pl.multiple_of(head * share, share), share), :]


def project(rows, place, pieces, wq, wk, wv, after=()):
    full, width = wq.shape
    share = rows // (full // width)
    tile = jax.ShapeDtypeStruct((rows, width), BF16)
    return call(
        first_kernel,
        (place, *pieces, wq, wk, wv),
        after,
        out_shape=(tile, tile, tile, jax.ShapeDtypeStruct((share, full), BF16), tile) + (jax.ShapeDtypeStruct(wq.shape, BF16),) * 3,
        in_specs=[SMEM] + [VMEM] * (len(pieces) + 3),
        out_specs=(VMEM,) * 8,
        scratch_shapes=[pltpu.VMEM((rows, full), BF16)],
        compiler_params=params(),
        cost_estimate=cost(6 * rows * full * width, 8 * full * width),
        name="project",
    )


def key_range(place, request, chunk, chunk_rows, tok_count):
    begin = jnp.int32(0)
    length = jnp.int32(0)
    for i in range(tok_count):
        begin += jnp.where(i < request, place[2 + i], 0)
        length += jnp.where(i == request, place[2 + i], 0)
    begin -= chunk * chunk_rows
    low = jnp.clip(begin, 0, chunk_rows)
    high = jnp.clip(begin + length, 0, chunk_rows)
    return low, high


def absorb(state, query, keys, values, valid):
    top, acc = state
    factor = math.log2(math.e) / math.sqrt(HEAD_DIM)
    scores = lax.dot_general(query, keys, (((1,), (1,)), ((), ())), preferred_element_type=F32)
    if valid is not None:
        scores = jnp.where(valid, scores, LOWEST)
    new_top = jnp.maximum(top, jnp.max(scores, axis=1, keepdims=True))
    weights = jnp.exp2((scores - new_top) * factor).astype(BF16)
    wide = jnp.concatenate([values, jnp.ones_like(values)], axis=1)
    acc = acc * jnp.exp2((top - new_top) * factor) + jnp.dot(weights, wide, preferred_element_type=F32)
    return new_top, acc


def cached_states(place, request, query, keys, values, tok_count):
    rows, width = query.shape
    chunk_rows = keys.shape[0]
    heads = width // HEAD_DIM
    span = min(512, chunk_rows)
    low, high = key_range(place, request, place[0], chunk_rows, tok_count)
    first = low // span
    last = jnp.where(high > low, (high + span - 1) // span, first)

    def step(block, states):
        start = pl.multiple_of(block * span, span)
        spots = start + lax.broadcasted_iota(jnp.int32, (rows, span), 1)
        valid = (spots >= low) & (spots < high)
        out = []
        for j in range(heads):
            cols = slice(j * HEAD_DIM, (j + 1) * HEAD_DIM)
            out.append(
                absorb(states[j], query[:, cols], keys[pl.ds(start, span), cols], values[pl.ds(start, span), cols], valid)
            )
        return tuple(out)

    empty = (jnp.full((rows, 1), LOWEST, F32), jnp.zeros((rows, 2 * HEAD_DIM), F32))
    return lax.fori_loop(first, last, step, (empty,) * heads)


def settle(state):
    top, acc = state
    total = acc[:, HEAD_DIM:]
    some = total > 0.0
    safe = jnp.where(some, total, 1.0)
    log_sum = jnp.where(some, top * (1.0 / math.sqrt(HEAD_DIM)) + jnp.log(safe), LOWEST)
    return acc[:, :HEAD_DIM] / safe, log_sum


def own_kernel(tok_count, place, query, new_keys, new_values, keys, values, mixed_out, log_out):
    states = cached_states(place, place[0], query, keys, values, tok_count)
    for j, state in enumerate(states):
        cols = slice(j * HEAD_DIM, (j + 1) * HEAD_DIM)
        state = absorb(state, query[:, cols], new_keys[:, cols], new_values[:, cols], None)
        mixed, log_sum = settle(state)
        mixed_out[:, cols] = mixed
        log_out[:, cols] = log_sum


def own_part(tok_count, place, query, new_keys, new_values, keys, values, after=()):
    rows, width = query.shape
    shape = jax.ShapeDtypeStruct((rows, width), F32)
    return call(
        functools.partial(own_kernel, tok_count),
        (place, query, new_keys, new_values, keys, values),
        after,
        out_shape=(shape, shape),
        in_specs=[SMEM] + [VMEM] * 5,
        out_specs=(VMEM, VMEM),
        compiler_params=params(),
        cost_estimate=cost(4 * rows * width * keys.shape[0], 4 * keys.shape[0] * width),
        name="own_part",
    )


def away_part(place, mask, query, keys, values, out, tok_count):
    rows, width = query.shape
    states = cached_states(place, jnp.bitwise_xor(place[0], mask), query, keys, values, tok_count)
    pieces = []
    for j, state in enumerate(states):
        mixed, log_sum = settle(state)
        out[:rows, j * HEAD_DIM : (j + 1) * HEAD_DIM] = mixed.astype(BF16)
        rest = jnp.transpose(log_sum)[:1, :]
        for _ in range(3):
            piece = rest.astype(BF16).astype(F32)
            pieces.append(piece)
            rest = rest - piece
    at = lax.broadcasted_iota(jnp.int32, (16, rows), 0)
    tail = jnp.zeros((16, rows), F32)
    for i, piece in enumerate(pieces):
        tail = jnp.where(at == i, piece, tail)
    out[rows : rows + 16, :] = tail.astype(BF16)


def second_kernel(tok_count, masks, place, *refs):
    count = len(masks)
    queries, (keys, values), refs = refs[:count], refs[count : count + 2], refs[count + 2 :]
    messages, x = refs[-5 - count : -5], refs[-1]
    project_kernel(place, *refs[: -5 - count], *refs[-5:-1], x)
    for mask, query, message in zip(masks, queries, messages, strict=True):
        away_part(place, mask, query, keys, values, message, tok_count)


def second_stage(tok_count, masks, place, queries, keys, values, pieces, wq, wk, wv, after=()):
    rows, width = queries[0].shape
    full = wq.shape[0]
    share = rows // (full // width)
    tile = jax.ShapeDtypeStruct((rows, width), BF16)
    message = jax.ShapeDtypeStruct((rows + 16, width), BF16)
    outs = (message,) * len(masks) + (tile, tile, tile, jax.ShapeDtypeStruct((share, full), BF16))
    results = call(
        functools.partial(second_kernel, tok_count, masks),
        (place, *queries, keys, values, *pieces, wq, wk, wv),
        after,
        out_shape=outs,
        in_specs=[SMEM] + [VMEM] * (len(masks) + len(pieces) + 5),
        out_specs=(VMEM,) * len(outs),
        scratch_shapes=[pltpu.VMEM((rows, full), BF16)],
        compiler_params=params(),
        cost_estimate=cost(4 * rows * width * keys.shape[0] + 6 * rows * full * width, 8 * full * width),
        name="second_stage",
    )
    return results[: len(masks)], results[len(masks) :]


def away_kernel(tok_count, masks, place, *refs):
    count = len(masks)
    queries, (keys, values), outs = refs[:count], refs[count : count + 2], refs[count + 2 :]
    for mask, query, out in zip(masks, queries, outs, strict=True):
        away_part(place, mask, query, keys, values, out, tok_count)


def away_parts(tok_count, masks, place, queries, keys, values, after=()):
    rows, width = queries[0].shape
    out = jax.ShapeDtypeStruct((rows + 16, width), BF16)
    return call(
        functools.partial(away_kernel, tok_count, masks),
        (place, *queries, keys, values),
        after,
        out_shape=(out,) * len(masks),
        in_specs=[SMEM] + [VMEM] * (len(masks) + 2),
        out_specs=(VMEM,) * len(masks),
        compiler_params=params(),
        cost_estimate=cost(4 * rows * width * keys.shape[0], 4 * keys.shape[0] * width),
        name="away_parts",
    )


def combine_kernel(share, place, mixed, logs, *refs):
    *messages, keep_out, send_out, whole = refs
    rows, width = mixed.shape
    tails = [message[rows : rows + 16, :].astype(F32) for message in messages]
    for j in range(width // HEAD_DIM):
        cols = slice(j * HEAD_DIM, (j + 1) * HEAD_DIM)
        parts = [(mixed[:, cols], logs[:, cols])]
        for message, tail in zip(messages, tails, strict=True):
            row = tail[3 * j : 3 * j + 1] + tail[3 * j + 1 : 3 * j + 2] + tail[3 * j + 2 : 3 * j + 3]
            log_sum = jnp.transpose(jnp.broadcast_to(row, (HEAD_DIM, rows)))
            parts.append((message[:rows, cols].astype(F32), log_sum))
        top = functools.reduce(jnp.maximum, [log_sum for _, log_sum in parts])
        total, acc = 0.0, 0.0
        for part, log_sum in parts:
            weight = jnp.exp(log_sum - top)
            total += weight
            acc += weight * part
        whole[:, cols] = (acc / total).astype(BF16)
    head = place[1]
    core = jnp.bitwise_and(head, 1)
    for slot in range(keep_out.shape[0] // share):
        pair = jnp.bitwise_xor(head, 2 * slot) - core
        at = pl.multiple_of((pair + core) * share, share)
        other = pl.multiple_of((pair + 1 - core) * share, share)
        keep_out[slot * share : (slot + 1) * share, :] = whole[pl.ds(at, share), :]
        send_out[slot * share : (slot + 1) * share, :] = whole[pl.ds(other, share), :]


def combine(share, place, mixed, logs, messages, after=()):
    rows, width = mixed.shape
    half = jax.ShapeDtypeStruct((rows // 2, width), BF16)
    return call(
        functools.partial(combine_kernel, share),
        (place, mixed, logs, *messages),
        after,
        out_shape=(half, half),
        in_specs=[SMEM] + [VMEM] * (len(messages) + 2),
        out_specs=(VMEM, VMEM),
        scratch_shapes=[pltpu.VMEM((rows, width), BF16)],
        compiler_params=params(),
        cost_estimate=cost(rows * width * 40, rows * width * 16),
        name="combine",
    )


def ids_kernel(tok_count, vocab_here, place, ids, local_out, owner_out):
    tiles = ids.shape[0] // tok_count
    for slot in range(tok_count):
        for tile in range(tiles):
            row = ids[pl.ds(jnp.bitwise_xor(place[0], slot) * tiles + tile, 1), :]
            at = slot * tiles + tile
            local_out[at : at + 1, :] = jnp.clip(row - place[0] * vocab_here, 0, vocab_here - 1)
            if slot == 0:
                owner = jnp.zeros(row.shape, jnp.int32)
                for i in range(1, tok_count):
                    owner += jnp.where(row >= i * vocab_here, 1, 0)
                owner_out[:, tile * 128 : (tile + 1) * 128] = owner


def sort_ids(tok_count, vocab_here, place, ids):
    ids = ids.reshape(-1, 128)
    local, owner = pl.pallas_call(
        functools.partial(ids_kernel, tok_count, vocab_here),
        out_shape=(
            jax.ShapeDtypeStruct(ids.shape, jnp.int32),
            jax.ShapeDtypeStruct((1, ids.size // tok_count), jnp.int32),
        ),
        in_specs=[SMEM, VMEM],
        out_specs=(VMEM, VMEM),
        compiler_params=params(),
        name="sort_ids",
    )(place, ids)
    return local.reshape(-1), owner


def choose_kernel(place, accept, owner, states, *refs):
    *found, out = refs
    rows = states.shape[0]
    slot = jnp.where(accept[...] == 1, jnp.bitwise_xor(owner[...], place[0]), len(found)).astype(F32)
    slot = jnp.transpose(jnp.broadcast_to(slot, (128, rows)))
    for start in range(0, states.shape[1], 128):
        cols = slice(start, start + 128)
        value = states[:, cols].astype(F32)
        for i, rows_found in enumerate(found):
            value = jnp.where(slot == i, rows_found[:, cols].astype(F32), value)
        out[:, cols] = value.astype(BF16)


def choose(place, accept, owner, states, found, after=()):
    return call(
        choose_kernel,
        (place, accept, owner, states, *found),
        after,
        out_shape=jax.ShapeDtypeStruct(states.shape, BF16),
        in_specs=[SMEM] + [VMEM] * (3 + len(found)),
        out_specs=VMEM,
        compiler_params=params(),
        name="choose",
    )


def stack_kernel(*refs):
    *pieces, out = refs
    at = 0
    for piece in pieces:
        out[at : at + piece.shape[0], :] = piece[...]
        at += piece.shape[0]


def stack(pieces, after=()):
    rows = sum(piece.shape[0] for piece in pieces)
    return call(
        stack_kernel,
        tuple(pieces),
        after,
        out_shape=jax.ShapeDtypeStruct((rows, pieces[0].shape[1]), BF16),
        in_specs=[VMEM] * len(pieces),
        out_specs=VMEM,
        compiler_params=params(),
        name="stack",
    )


def out_kernel(keep, other, w_keep, w_other, *outs):
    share = outs[0].shape[0]
    total = jnp.dot(other[...], w_other[...], preferred_element_type=F32)
    total += jnp.dot(keep[...], w_keep[...], preferred_element_type=F32)
    for slot, out in enumerate(outs):
        out[...] = total[slot * share : (slot + 1) * share].astype(out.dtype)


def out_project(share, keep, other, w_keep, w_other):
    half, width = keep.shape
    full = w_keep.shape[1]
    return pl.pallas_call(
        out_kernel,
        out_shape=tuple(jax.ShapeDtypeStruct((share, full), F32 if s == 0 else BF16) for s in range(half // share)),
        in_specs=[VMEM] * 4,
        out_specs=(VMEM,) * (half // share),
        compiler_params=params(),
        cost_estimate=cost(4 * half * width * full, 4 * width * full),
        name="out_project",
    )(keep, other, w_keep, w_other)


def finish_kernel(last, own, *refs):
    *refs, attn_gain, final_gain, sems = refs
    *others, residual, attn_far, final_far, first_out = refs[: len(refs) - (0 if last else 2)]
    copies = fetch((attn_far, final_far), (attn_gain, final_gain), sems)
    total = own[...]
    for other in others:
        total += other[...].astype(F32)
    scale = lax.rsqrt(jnp.mean(total * total, axis=1, keepdims=True) + EPSILON)
    for copy in copies:
        copy.wait()
    first = (residual[...].astype(F32) + total * scale * attn_gain[...]).astype(BF16)
    first_out[...] = first
    if not last:
        normed_out, square_out = refs[-2:]
        wide = first.astype(F32)
        squares = jnp.sum(wide * wide, axis=1, keepdims=True)
        scale = lax.rsqrt(squares / wide.shape[1] + EPSILON)
        normed_out[...] = (wide * scale * final_gain[...]).astype(BF16)
        square_out[...] = jnp.broadcast_to(jnp.sum(squares, axis=0, keepdims=True), square_out.shape)


def finish(last, own, others, residual, attn_gain, final_gain, after=()):
    state = jax.ShapeDtypeStruct(residual.shape, BF16)
    outs = (state,) if last else (state, state, jax.ShapeDtypeStruct((1, 128), F32))
    return call(
        functools.partial(finish_kernel, last),
        (own, *others, residual, attn_gain, final_gain),
        after,
        out_shape=outs,
        in_specs=[VMEM] * (len(others) + 2) + [HBM] * 2,
        out_specs=(VMEM,) * len(outs),
        scratch_shapes=[pltpu.VMEM(attn_gain.shape, F32)] * 2 + [pltpu.SemaphoreType.DMA((2,))],
        compiler_params=params(),
        cost_estimate=cost(residual.size * 20, residual.size * 12),
        name="finish",
    )


def hand_on_kernel(first, second, *outs):
    half = first.shape[0] // 2
    outs[0][...] = first[...]
    outs[1][...] = second[...]
    outs[2][...] = second[:half, :]
    outs[3][...] = first[half:, :]


def hand_on(first, second, after=()):
    whole = jax.ShapeDtypeStruct(first.shape, BF16)
    half = jax.ShapeDtypeStruct((first.shape[0] // 2, first.shape[1]), BF16)
    return call(
        hand_on_kernel,
        (first, second),
        after,
        out_shape=(whole, whole, half, half),
        in_specs=[VMEM] * 2,
        out_specs=(VMEM,) * 4,
        compiler_params=params(),
        name="hand_on",
    )


def logits_kernel(share, tok_count, place, mine, other, lm_block, best_out, x):
    @pl.when(pl.program_id(0) == 0)
    def _():
        core = jnp.bitwise_and(place[1], 1)
        for flag, piece in enumerate((mine, other)):
            for slot in range(tok_count):
                tok = jnp.bitwise_xor(place[0], slot)
                at = pl.multiple_of((2 * tok + jnp.bitwise_xor(core, flag)) * share, share)
                x[pl.ds(at, share), :] = piece[slot * share : (slot + 1) * share, :]
        best_out[...] = jnp.full(best_out.shape, -jnp.inf, F32)

    logits = lax.dot_general(lm_block[...], x[...], (((1,), (1,)), ((), ())), preferred_element_type=F32)
    best = jnp.max(logits.reshape(logits.shape[0] // 8, 8, logits.shape[1]), axis=0)
    best_out[...] = jnp.maximum(best_out[...], best)


def largest_logits(share, tok_count, place, mine, other, lm_head, after=()):
    half, full = mine.shape
    vocab = lm_head.shape[0]
    span = vocab // 4 if vocab % 64 == 0 else vocab // 7
    return call(
        functools.partial(logits_kernel, share, tok_count),
        (place, mine, other, lm_head),
        after,
        out_shape=jax.ShapeDtypeStruct((8, 2 * half), F32),
        grid=(vocab // span,),
        in_specs=[SMEM, VMEM, VMEM, pl.BlockSpec((span, full), lambda i: (i, 0))],
        out_specs=VMEM,
        scratch_shapes=[pltpu.VMEM((2 * half, full), BF16)],
        compiler_params=params(),
        cost_estimate=cost(4 * half * full * vocab, 2 * full * vocab),
        name="largest_logits",
    )


def gather_best_kernel(place, square, *refs):
    *bests, out = refs
    chip = place[1] // 2
    out[...] = jnp.zeros(out.shape, F32)
    for slot, best in enumerate(bests):
        out[pl.ds(jnp.bitwise_xor(chip, slot), 1), :] = jnp.max(best[...], axis=0, keepdims=True)
    lanes = lax.broadcasted_iota(jnp.int32, (1, out.shape[1]), 1)
    out[len(bests) : len(bests) + 1, :] = jnp.where(lanes == place[0], square[:, :1], 0.0)


def gather_best(place, square, bests):
    rows = -(-(len(bests) + 1) // 8) * 8
    return pl.pallas_call(
        gather_best_kernel,
        out_shape=jax.ShapeDtypeStruct((rows, bests[0].shape[1]), F32),
        in_specs=[SMEM] + [VMEM] * (1 + len(bests)),
        out_specs=VMEM,
        compiler_params=params(),
        name="gather_best",
    )(place, square, *bests)


def shards(
    block_states,
    token_ids,
    accept,
    cache_lengths,
    cache_keys,
    cache_values,
    w_query,
    w_key,
    w_value,
    w_out,
    attn_gain,
    final_gain,
    embed,
    lm_head,
):
    tok_index = lax.axis_index("tok")
    head_index = lax.axis_index("head")
    tok_count = lax.axis_size("tok")
    head_count = lax.axis_size("head")
    chips = head_count // 2
    block_rows = block_states.shape[0]
    share = block_rows // head_count
    model_width = w_query.shape[0]
    place = jnp.concatenate([jnp.stack([tok_index, head_index]).astype(jnp.int32), cache_lengths])
    gains = (attn_gain.reshape(1, -1), final_gain.reshape(1, -1))
    tok_masks = range(1, tok_count)

    def by_head(value, mask):
        return lax.ppermute(value, "head", xor_pairs(head_count, mask))

    def by_tok(value, mask):
        return lax.ppermute(value, "tok", xor_pairs(tok_count, mask))

    def spread(features):
        pieces = [features] + [by_head(features, 2 * s) for s in range(1, chips)]
        return pieces, [by_head(piece, 1) for piece in pieces]

    def exchange(arrays):
        return [by_tok(array, mask) for mask, array in zip(tok_masks, arrays, strict=True)]

    def join(own, messages, after=()):
        return combine(share, place, *own, messages, after)

    def out_layer(keep, send):
        return out_project(share, keep, by_head(send, 1), w_out, w_out_other)

    def finish_layer(last, sums, residual, after=()):
        own, *others = sums
        others = [by_head(total, 2 * s) for s, total in enumerate(others, 1)]
        return finish(last, own, others, residual, *gains, after)


    w_out_other = by_head(w_out, 1)

    vocab_here = embed.shape[0]
    ids, owners = sort_ids(tok_count, vocab_here, place, token_ids)
    found = embed.at[ids].get(mode="promise_in_bounds").reshape(tok_count, block_rows, -1)
    found = [found[mask] for mask in range(tok_count)]
    embedded = [found[0], *exchange(found[1:])]

    pieces, others = spread(block_states)
    query, key, value, residual, states, *weights = project(
        block_rows, place, pieces + others, w_query, w_key, w_value, [w_out_other, found[1]]
    )
    queries = exchange([query] * len(tok_masks))
    cache_keys, cache_values = carry(cache_keys, cache_values)
    own = own_part(tok_count, place, query, key, value, cache_keys, cache_values)
    chosen = choose(place, accept.reshape(1, -1), owners, states, embedded, queries[:1])
    pieces, others = spread(chosen)
    messages, (query, key, value, residual_two) = second_stage(
        tok_count, tok_masks, place, queries, cache_keys, cache_values, pieces + others, *weights
    )
    messages = exchange(messages)
    queries = exchange([query] * len(tok_masks))
    own_two = own_part(tok_count, place, query, key, value, cache_keys, cache_values)
    keep = join(own, messages, [own_two[0]])
    parts = away_parts(tok_count, tok_masks, place, queries, cache_keys, cache_values, [keep[0]])
    _, normed, square = finish_layer(False, out_layer(*keep), residual, parts[:1])

    column = stack([normed] + exchange([normed] * len(tok_masks)))
    parts = exchange(parts)

    def best_of(piece, after=()):
        return largest_logits(share, tok_count, place, piece, by_head(piece, 1), lm_head, after)

    bests = [best_of(column)]
    if chips == 4:
        along_x, along_y, along_y_half, along_x_half = hand_on(
            by_head(column, 2), by_head(column, 4), [bests[0], *parts]
        )
        bests.append(best_of(along_x))
        bests.append(best_of(along_y, bests[1:]))
        across = stack([by_head(along_y_half, 2), by_head(along_x_half, 4)], bests[2:])
        bests.append(best_of(across))
    else:
        for s in range(1, chips):
            bests.append(best_of(by_head(column, 2 * s), bests[-1:]))
    sums = out_layer(*join(own_two, parts))
    (hiddens,) = finish_layer(True, sums, residual_two)

    best = gather_best(place, square, bests)
    is_max = lax.broadcasted_iota(jnp.int32, best.shape, 0) < chips
    for axis, size in (("head", head_count), ("tok", tok_count)):
        mask = 1
        while mask < size:
            other = lax.ppermute(best, axis, xor_pairs(size, mask))
            best = jnp.where(is_max, jnp.maximum(best, other), best + other)
            mask *= 2
    top_logits = best[:chips].reshape(chips, tok_count, 2, share).transpose(1, 0, 2, 3).reshape(-1)
    request_norms = jnp.sqrt(best[chips, :tok_count] / (block_rows * model_width))
    return (hiddens, request_norms, top_logits)


def solution(mesh):
    placed = (
        P("tok", "head"),
        P(),
        P("tok"),
        P(),
        P("tok", "head"),
        P("tok", "head"),
        P(None, "head"),
        P(None, "head"),
        P(None, "head"),
        P("head", None),
        P(),
        P(),
        P("tok", "head"),
        P(("tok", "head"), None),
    )
    return jax.shard_map(
        shards,
        mesh=mesh,
        in_specs=placed,
        out_specs=(P(("tok", "head"), None), P(), P()),
        check_vma=False,
    )
```

```python
import functools
import math

import jax
import jax.numpy as jnp
from jax import lax
from jax.experimental import pallas as pl
from jax.experimental.pallas import tpu as pltpu
from jax.sharding import PartitionSpec as P

HEAD_DIM = 128
EPSILON = 1e-06
LOWEST = -1e30
BF16 = jnp.bfloat16
F32 = jnp.float32

SMEM = pl.BlockSpec(memory_space=pltpu.SMEM)
VMEM = pl.BlockSpec(memory_space=pltpu.VMEM)
HBM = pl.BlockSpec(memory_space=pltpu.HBM)


def params(mib=24):
    return pltpu.CompilerParams(vmem_limit_bytes=mib * 2**20)


def cost(flops, moved):
    return pl.CostEstimate(flops=flops, bytes_accessed=moved, transcendentals=0)


def call(kernel, operands, after=(), in_specs=None, **rest):
    count = len(operands)

    def body(*refs):
        kernel(*refs[:count], *refs[count + len(after) :])

    specs = list(in_specs) + [pl.BlockSpec(memory_space=pl.ANY)] * len(after)
    return pl.pallas_call(body, in_specs=specs, **rest)(*operands, *after)


def xor_pairs(size, mask):
    return [(i, i ^ mask) for i in range(size)]


def fetch(sources, targets, sems):
    copies = [pltpu.make_async_copy(a, b, sems.at[i]) for i, (a, b) in enumerate(zip(sources, targets, strict=True))]
    for copy in copies:
        copy.start()
    return copies


def carry_kernel(*refs):
    count = len(refs) // 2
    for source, out in zip(refs[:count], refs[count:], strict=True):
        out[...] = source[...]


def carry(*arrays):
    return pl.pallas_call(
        carry_kernel,
        out_shape=tuple(jax.ShapeDtypeStruct(a.shape, a.dtype) for a in arrays),
        in_specs=[VMEM] * len(arrays),
        out_specs=(VMEM,) * len(arrays),
        compiler_params=params(),
        name="carry",
    )(*arrays)


def first_kernel(place, *refs):
    project_kernel(place, *refs[:-5], refs[-1])
    for source, out in zip((refs[0], *refs[-12:-9]), refs[-5:-1], strict=True):
        out[...] = source[...]


def project_kernel(place, *refs):
    *pieces, wq, wk, wv, q_out, k_out, v_out, res_out, x = refs
    head = place[1]
    rows, width = q_out.shape
    for odd in range(2):
        mask = odd
        for piece in pieces[odd * len(pieces) // 2 : (odd + 1) * len(pieces) // 2]:
            for start in range(0, piece.shape[0], rows):
                at = pl.multiple_of(jnp.bitwise_xor(head, mask) * width, width)
                x[:, pl.ds(at, width)] = piece[start : start + rows, :]
                mask += 2
    for w, out in ((wq, q_out), (wk, k_out), (wv, v_out)):
        out[...] = jnp.dot(x[...], w[...], preferred_element_type=F32).astype(BF16)
    share = res_out.shape[0]
    res_out[...] = x[pl.ds(pl.multiple_of(head * share, share), share), :]


def project(rows, place, pieces, wq, wk, wv, after=()):
    full, width = wq.shape
    share = rows // (full // width)
    tile = jax.ShapeDtypeStruct((rows, width), BF16)
    return call(
        first_kernel,
        (place, *pieces, wq, wk, wv),
        after,
        out_shape=(tile, tile, tile, jax.ShapeDtypeStruct((share, full), BF16), tile) + (jax.ShapeDtypeStruct(wq.shape, BF16),) * 3,
        in_specs=[SMEM] + [VMEM] * (len(pieces) + 3),
        out_specs=(VMEM,) * 8,
        scratch_shapes=[pltpu.VMEM((rows, full), BF16)],
        compiler_params=params(),
        cost_estimate=cost(6 * rows * full * width, 8 * full * width),
        name="project",
    )


def key_range(place, request, chunk, chunk_rows, tok_count):
    begin = jnp.int32(0)
    length = jnp.int32(0)
    for i in range(tok_count):
        begin += jnp.where(i < request, place[2 + i], 0)
        length += jnp.where(i == request, place[2 + i], 0)
    begin -= chunk * chunk_rows
    low = jnp.clip(begin, 0, chunk_rows)
    high = jnp.clip(begin + length, 0, chunk_rows)
    return low, high


def absorb(state, query, keys, values, valid):
    top, acc = state
    factor = math.log2(math.e) / math.sqrt(HEAD_DIM)
    scores = lax.dot_general(query, keys, (((1,), (1,)), ((), ())), preferred_element_type=F32)
    if valid is not None:
        scores = jnp.where(valid, scores, LOWEST)
    new_top = jnp.maximum(top, jnp.max(scores, axis=1, keepdims=True))
    weights = jnp.exp2((scores - new_top) * factor).astype(BF16)
    wide = jnp.concatenate([values, jnp.ones_like(values)], axis=1)
    acc = acc * jnp.exp2((top - new_top) * factor) + jnp.dot(weights, wide, preferred_element_type=F32)
    return new_top, acc


def cached_states(place, request, query, keys, values, tok_count):
    rows, width = query.shape
    chunk_rows = keys.shape[0]
    heads = width // HEAD_DIM
    span = min(512, chunk_rows)
    low, high = key_range(place, request, place[0], chunk_rows, tok_count)
    first = low // span
    last = jnp.where(high > low, (high + span - 1) // span, first)

    def step(block, states):
        start = pl.multiple_of(block * span, span)
        spots = start + lax.broadcasted_iota(jnp.int32, (rows, span), 1)
        valid = (spots >= low) & (spots < high)
        out = []
        for j in range(heads):
            cols = slice(j * HEAD_DIM, (j + 1) * HEAD_DIM)
            out.append(
                absorb(states[j], query[:, cols], keys[pl.ds(start, span), cols], values[pl.ds(start, span), cols], valid)
            )
        return tuple(out)

    empty = (jnp.full((rows, 1), LOWEST, F32), jnp.zeros((rows, 2 * HEAD_DIM), F32))
    return lax.fori_loop(first, last, step, (empty,) * heads)


def settle(state):
    top, acc = state
    total = acc[:, HEAD_DIM:]
    some = total > 0.0
    safe = jnp.where(some, total, 1.0)
    log_sum = jnp.where(some, top * (1.0 / math.sqrt(HEAD_DIM)) + jnp.log(safe), LOWEST)
    return acc[:, :HEAD_DIM] / safe, log_sum


def own_kernel(tok_count, place, query, new_keys, new_values, keys, values, mixed_out, log_out):
    states = cached_states(place, place[0], query, keys, values, tok_count)
    for j, state in enumerate(states):
        cols = slice(j * HEAD_DIM, (j + 1) * HEAD_DIM)
        state = absorb(state, query[:, cols], new_keys[:, cols], new_values[:, cols], None)
        mixed, log_sum = settle(state)
        mixed_out[:, cols] = mixed
        log_out[:, cols] = log_sum


def own_part(tok_count, place, query, new_keys, new_values, keys, values, after=()):
    rows, width = query.shape
    shape = jax.ShapeDtypeStruct((rows, width), F32)
    return call(
        functools.partial(own_kernel, tok_count),
        (place, query, new_keys, new_values, keys, values),
        after,
        out_shape=(shape, shape),
        in_specs=[SMEM] + [VMEM] * 5,
        out_specs=(VMEM, VMEM),
        compiler_params=params(),
        cost_estimate=cost(4 * rows * width * keys.shape[0], 4 * keys.shape[0] * width),
        name="own_part",
    )


def away_part(place, mask, query, keys, values, out, tok_count):
    rows, width = query.shape
    states = cached_states(place, jnp.bitwise_xor(place[0], mask), query, keys, values, tok_count)
    pieces = []
    for j, state in enumerate(states):
        mixed, log_sum = settle(state)
        out[:rows, j * HEAD_DIM : (j + 1) * HEAD_DIM] = mixed.astype(BF16)
        rest = jnp.transpose(log_sum)[:1, :]
        for _ in range(3):
            piece = rest.astype(BF16).astype(F32)
            pieces.append(piece)
            rest = rest - piece
    at = lax.broadcasted_iota(jnp.int32, (16, rows), 0)
    tail = jnp.zeros((16, rows), F32)
    for i, piece in enumerate(pieces):
        tail = jnp.where(at == i, piece, tail)
    out[rows : rows + 16, :] = tail.astype(BF16)


def second_kernel(tok_count, masks, place, *refs):
    count = len(masks)
    queries, (keys, values), refs = refs[:count], refs[count : count + 2], refs[count + 2 :]
    messages, x = refs[-5 - count : -5], refs[-1]
    project_kernel(place, *refs[: -5 - count], *refs[-5:-1], x)
    for mask, query, message in zip(masks, queries, messages, strict=True):
        away_part(place, mask, query, keys, values, message, tok_count)


def second_stage(tok_count, masks, place, queries, keys, values, pieces, wq, wk, wv, after=()):
    rows, width = queries[0].shape
    full = wq.shape[0]
    share = rows // (full // width)
    tile = jax.ShapeDtypeStruct((rows, width), BF16)
    message = jax.ShapeDtypeStruct((rows + 16, width), BF16)
    outs = (message,) * len(masks) + (tile, tile, tile, jax.ShapeDtypeStruct((share, full), BF16))
    results = call(
        functools.partial(second_kernel, tok_count, masks),
        (place, *queries, keys, values, *pieces, wq, wk, wv),
        after,
        out_shape=outs,
        in_specs=[SMEM] + [VMEM] * (len(masks) + len(pieces) + 5),
        out_specs=(VMEM,) * len(outs),
        scratch_shapes=[pltpu.VMEM((rows, full), BF16)],
        compiler_params=params(),
        cost_estimate=cost(4 * rows * width * keys.shape[0] + 6 * rows * full * width, 8 * full * width),
        name="second_stage",
    )
    return results[: len(masks)], results[len(masks) :]


def away_kernel(tok_count, masks, place, *refs):
    count = len(masks)
    queries, (keys, values), outs = refs[:count], refs[count : count + 2], refs[count + 2 :]
    for mask, query, out in zip(masks, queries, outs, strict=True):
        away_part(place, mask, query, keys, values, out, tok_count)


def away_parts(tok_count, masks, place, queries, keys, values, after=()):
    rows, width = queries[0].shape
    out = jax.ShapeDtypeStruct((rows + 16, width), BF16)
    return call(
        functools.partial(away_kernel, tok_count, masks),
        (place, *queries, keys, values),
        after,
        out_shape=(out,) * len(masks),
        in_specs=[SMEM] + [VMEM] * (len(masks) + 2),
        out_specs=(VMEM,) * len(masks),
        compiler_params=params(),
        cost_estimate=cost(4 * rows * width * keys.shape[0], 4 * keys.shape[0] * width),
        name="away_parts",
    )


def combine_kernel(share, place, mixed, logs, *refs):
    *messages, keep_out, send_out, whole = refs
    rows, width = mixed.shape
    tails = [message[rows : rows + 16, :].astype(F32) for message in messages]
    for j in range(width // HEAD_DIM):
        cols = slice(j * HEAD_DIM, (j + 1) * HEAD_DIM)
        parts = [(mixed[:, cols], logs[:, cols])]
        for message, tail in zip(messages, tails, strict=True):
            row = tail[3 * j : 3 * j + 1] + tail[3 * j + 1 : 3 * j + 2] + tail[3 * j + 2 : 3 * j + 3]
            log_sum = jnp.transpose(jnp.broadcast_to(row, (HEAD_DIM, rows)))
            parts.append((message[:rows, cols].astype(F32), log_sum))
        top = functools.reduce(jnp.maximum, [log_sum for _, log_sum in parts])
        total, acc = 0.0, 0.0
        for part, log_sum in parts:
            weight = jnp.exp(log_sum - top)
            total += weight
            acc += weight * part
        whole[:, cols] = (acc / total).astype(BF16)
    head = place[1]
    core = jnp.bitwise_and(head, 1)
    for slot in range(keep_out.shape[0] // share):
        pair = jnp.bitwise_xor(head, 2 * slot) - core
        at = pl.multiple_of((pair + core) * share, share)
        other = pl.multiple_of((pair + 1 - core) * share, share)
        keep_out[slot * share : (slot + 1) * share, :] = whole[pl.ds(at, share), :]
        send_out[slot * share : (slot + 1) * share, :] = whole[pl.ds(other, share), :]


def combine(share, place, mixed, logs, messages, after=()):
    rows, width = mixed.shape
    half = jax.ShapeDtypeStruct((rows // 2, width), BF16)
    return call(
        functools.partial(combine_kernel, share),
        (place, mixed, logs, *messages),
        after,
        out_shape=(half, half),
        in_specs=[SMEM] + [VMEM] * (len(messages) + 2),
        out_specs=(VMEM, VMEM),
        scratch_shapes=[pltpu.VMEM((rows, width), BF16)],
        compiler_params=params(),
        cost_estimate=cost(rows * width * 40, rows * width * 16),
        name="combine",
    )


def ids_kernel(tok_count, vocab_here, place, ids, local_out, owner_out):
    tiles = ids.shape[0] // tok_count
    for slot in range(tok_count):
        for tile in range(tiles):
            row = ids[pl.ds(jnp.bitwise_xor(place[0], slot) * tiles + tile, 1), :]
            at = slot * tiles + tile
            local_out[at : at + 1, :] = jnp.clip(row - place[0] * vocab_here, 0, vocab_here - 1)
            if slot == 0:
                owner = jnp.zeros(row.shape, jnp.int32)
                for i in range(1, tok_count):
                    owner += jnp.where(row >= i * vocab_here, 1, 0)
                owner_out[:, tile * 128 : (tile + 1) * 128] = owner


def sort_ids(tok_count, vocab_here, place, ids):
    ids = ids.reshape(-1, 128)
    local, owner = pl.pallas_call(
        functools.partial(ids_kernel, tok_count, vocab_here),
        out_shape=(
            jax.ShapeDtypeStruct(ids.shape, jnp.int32),
            jax.ShapeDtypeStruct((1, ids.size // tok_count), jnp.int32),
        ),
        in_specs=[SMEM, VMEM],
        out_specs=(VMEM, VMEM),
        compiler_params=params(),
        name="sort_ids",
    )(place, ids)
    return local.reshape(-1), owner


def choose_kernel(place, accept, owner, states, *refs):
    *found, out = refs
    rows = states.shape[0]
    slot = jnp.where(accept[...] == 1, jnp.bitwise_xor(owner[...], place[0]), len(found)).astype(F32)
    slot = jnp.transpose(jnp.broadcast_to(slot, (128, rows)))
    for start in range(0, states.shape[1], 128):
        cols = slice(start, start + 128)
        value = states[:, cols].astype(F32)
        for i, rows_found in enumerate(found):
            value = jnp.where(slot == i, rows_found[:, cols].astype(F32), value)
        out[:, cols] = value.astype(BF16)


def choose(place, accept, owner, states, found, after=()):
    return call(
        choose_kernel,
        (place, accept, owner, states, *found),
        after,
        out_shape=jax.ShapeDtypeStruct(states.shape, BF16),
        in_specs=[SMEM] + [VMEM] * (3 + len(found)),
        out_specs=VMEM,
        compiler_params=params(),
        name="choose",
    )


def stack_kernel(*refs):
    *pieces, out = refs
    at = 0
    for piece in pieces:
        out[at : at + piece.shape[0], :] = piece[...]
        at += piece.shape[0]


def stack(pieces, after=()):
    rows = sum(piece.shape[0] for piece in pieces)
    return call(
        stack_kernel,
        tuple(pieces),
        after,
        out_shape=jax.ShapeDtypeStruct((rows, pieces[0].shape[1]), BF16),
        in_specs=[VMEM] * len(pieces),
        out_specs=VMEM,
        compiler_params=params(),
        name="stack",
    )


def out_kernel(keep, other, w_keep, w_other, *outs):
    share = outs[0].shape[0]
    total = jnp.dot(other[...], w_other[...], preferred_element_type=F32)
    total += jnp.dot(keep[...], w_keep[...], preferred_element_type=F32)
    for slot, out in enumerate(outs):
        out[...] = total[slot * share : (slot + 1) * share].astype(out.dtype)


def out_project(share, keep, other, w_keep, w_other):
    half, width = keep.shape
    full = w_keep.shape[1]
    return pl.pallas_call(
        out_kernel,
        out_shape=tuple(jax.ShapeDtypeStruct((share, full), F32 if s == 0 else BF16) for s in range(half // share)),
        in_specs=[VMEM] * 4,
        out_specs=(VMEM,) * (half // share),
        compiler_params=params(),
        cost_estimate=cost(4 * half * width * full, 4 * width * full),
        name="out_project",
    )(keep, other, w_keep, w_other)


def finish_kernel(last, own, *refs):
    *refs, attn_gain, final_gain, sems = refs
    *others, residual, attn_far, final_far, first_out = refs[: len(refs) - (0 if last else 2)]
    copies = fetch((attn_far, final_far), (attn_gain, final_gain), sems)
    total = own[...]
    for other in others:
        total += other[...].astype(F32)
    scale = lax.rsqrt(jnp.mean(total * total, axis=1, keepdims=True) + EPSILON)
    for copy in copies:
        copy.wait()
    first = (residual[...].astype(F32) + total * scale * attn_gain[...]).astype(BF16)
    first_out[...] = first
    if not last:
        normed_out, square_out = refs[-2:]
        wide = first.astype(F32)
        squares = jnp.sum(wide * wide, axis=1, keepdims=True)
        scale = lax.rsqrt(squares / wide.shape[1] + EPSILON)
        normed_out[...] = (wide * scale * final_gain[...]).astype(BF16)
        square_out[...] = jnp.broadcast_to(jnp.sum(squares, axis=0, keepdims=True), square_out.shape)


def finish(last, own, others, residual, attn_gain, final_gain, after=()):
    state = jax.ShapeDtypeStruct(residual.shape, BF16)
    outs = (state,) if last else (state, state, jax.ShapeDtypeStruct((1, 128), F32))
    return call(
        functools.partial(finish_kernel, last),
        (own, *others, residual, attn_gain, final_gain),
        after,
        out_shape=outs,
        in_specs=[VMEM] * (len(others) + 2) + [HBM] * 2,
        out_specs=(VMEM,) * len(outs),
        scratch_shapes=[pltpu.VMEM(attn_gain.shape, F32)] * 2 + [pltpu.SemaphoreType.DMA((2,))],
        compiler_params=params(),
        cost_estimate=cost(residual.size * 20, residual.size * 12),
        name="finish",
    )


def hand_on_kernel(first, second, *outs):
    half = first.shape[0] // 2
    outs[0][...] = first[...]
    outs[1][...] = second[...]
    outs[2][...] = second[:half, :]
    outs[3][...] = first[half:, :]


def hand_on(first, second, after=()):
    whole = jax.ShapeDtypeStruct(first.shape, BF16)
    half = jax.ShapeDtypeStruct((first.shape[0] // 2, first.shape[1]), BF16)
    return call(
        hand_on_kernel,
        (first, second),
        after,
        out_shape=(whole, whole, half, half),
        in_specs=[VMEM] * 2,
        out_specs=(VMEM,) * 4,
        compiler_params=params(),
        name="hand_on",
    )


def logits_kernel(share, tok_count, place, mine, other, lm_block, best_out, x):
    @pl.when(pl.program_id(0) == 0)
    def _():
        core = jnp.bitwise_and(place[1], 1)
        for flag, piece in enumerate((mine, other)):
            for slot in range(tok_count):
                tok = jnp.bitwise_xor(place[0], slot)
                at = pl.multiple_of((2 * tok + jnp.bitwise_xor(core, flag)) * share, share)
                x[pl.ds(at, share), :] = piece[slot * share : (slot + 1) * share, :]
        best_out[...] = jnp.full(best_out.shape, -jnp.inf, F32)

    logits = lax.dot_general(lm_block[...], x[...], (((1,), (1,)), ((), ())), preferred_element_type=F32)
    best = jnp.max(logits.reshape(logits.shape[0] // 8, 8, logits.shape[1]), axis=0)
    best_out[...] = jnp.maximum(best_out[...], best)


def largest_logits(share, tok_count, place, mine, other, lm_head, after=()):
    half, full = mine.shape
    vocab = lm_head.shape[0]
    span = vocab // 2 if vocab % 32 == 0 else vocab // 7
    return call(
        functools.partial(logits_kernel, share, tok_count),
        (place, mine, other, lm_head),
        after,
        out_shape=jax.ShapeDtypeStruct((8, 2 * half), F32),
        grid=(vocab // span,),
        in_specs=[SMEM, VMEM, VMEM, pl.BlockSpec((span, full), lambda i: (i, 0))],
        out_specs=VMEM,
        scratch_shapes=[pltpu.VMEM((2 * half, full), BF16)],
        compiler_params=params(),
        cost_estimate=cost(4 * half * full * vocab, 2 * full * vocab),
        name="largest_logits",
    )


def gather_best_kernel(place, square, *refs):
    *bests, out = refs
    chip = place[1] // 2
    out[...] = jnp.zeros(out.shape, F32)
    for slot, best in enumerate(bests):
        out[pl.ds(jnp.bitwise_xor(chip, slot), 1), :] = jnp.max(best[...], axis=0, keepdims=True)
    lanes = lax.broadcasted_iota(jnp.int32, (1, out.shape[1]), 1)
    out[len(bests) : len(bests) + 1, :] = jnp.where(lanes == place[0], square[:, :1], 0.0)


def gather_best(place, square, bests):
    rows = -(-(len(bests) + 1) // 8) * 8
    return pl.pallas_call(
        gather_best_kernel,
        out_shape=jax.ShapeDtypeStruct((rows, bests[0].shape[1]), F32),
        in_specs=[SMEM] + [VMEM] * (1 + len(bests)),
        out_specs=VMEM,
        compiler_params=params(),
        name="gather_best",
    )(place, square, *bests)


def shards(
    block_states,
    token_ids,
    accept,
    cache_lengths,
    cache_keys,
    cache_values,
    w_query,
    w_key,
    w_value,
    w_out,
    attn_gain,
    final_gain,
    embed,
    lm_head,
):
    tok_index = lax.axis_index("tok")
    head_index = lax.axis_index("head")
    tok_count = lax.axis_size("tok")
    head_count = lax.axis_size("head")
    chips = head_count // 2
    block_rows = block_states.shape[0]
    share = block_rows // head_count
    model_width = w_query.shape[0]
    place = jnp.concatenate([jnp.stack([tok_index, head_index]).astype(jnp.int32), cache_lengths])
    gains = (attn_gain.reshape(1, -1), final_gain.reshape(1, -1))
    tok_masks = range(1, tok_count)

    def by_head(value, mask):
        return lax.ppermute(value, "head", xor_pairs(head_count, mask))

    def by_tok(value, mask):
        return lax.ppermute(value, "tok", xor_pairs(tok_count, mask))

    def spread(features):
        pieces = [features] + [by_head(features, 2 * s) for s in range(1, chips)]
        return pieces, [by_head(piece, 1) for piece in pieces]

    def exchange(arrays):
        return [by_tok(array, mask) for mask, array in zip(tok_masks, arrays, strict=True)]

    def join(own, messages, after=()):
        return combine(share, place, *own, messages, after)

    def out_layer(keep, send):
        return out_project(share, keep, by_head(send, 1), w_out, w_out_other)

    def finish_layer(last, sums, residual, after=()):
        own, *others = sums
        others = [by_head(total, 2 * s) for s, total in enumerate(others, 1)]
        return finish(last, own, others, residual, *gains, after)


    w_out_other = by_head(w_out, 1)

    vocab_here = embed.shape[0]
    ids, owners = sort_ids(tok_count, vocab_here, place, token_ids)
    found = embed.at[ids].get(mode="promise_in_bounds").reshape(tok_count, block_rows, -1)
    found = [found[mask] for mask in range(tok_count)]
    embedded = [found[0], *exchange(found[1:])]

    pieces, others = spread(block_states)
    query, key, value, residual, states, *weights = project(
        block_rows, place, pieces + others, w_query, w_key, w_value, [w_out_other, found[1]]
    )
    queries = exchange([query] * len(tok_masks))
    cache_keys, cache_values, accepted = carry(cache_keys, cache_values, accept.reshape(1, -1))
    own = own_part(tok_count, place, query, key, value, cache_keys, cache_values)
    chosen = choose(place, accepted, owners, states, embedded, queries[:1])
    pieces, others = spread(chosen)
    messages, (query, key, value, residual_two) = second_stage(
        tok_count, tok_masks, place, queries, cache_keys, cache_values, pieces + others, *weights
    )
    messages = exchange(messages)
    queries = exchange([query] * len(tok_masks))
    own_two = own_part(tok_count, place, query, key, value, cache_keys, cache_values)
    keep = join(own, messages, [own_two[0]])
    parts = away_parts(tok_count, tok_masks, place, queries, cache_keys, cache_values, [keep[0]])
    _, normed, square = finish_layer(False, out_layer(*keep), residual)

    column = stack([normed] + exchange([normed] * len(tok_masks)), parts[:1])
    parts = exchange(parts)

    def best_of(piece, after=()):
        return largest_logits(share, tok_count, place, piece, by_head(piece, 1), lm_head, after)

    bests = [best_of(column)]
    if chips == 4:
        along_x, along_y, along_y_half, along_x_half = hand_on(
            by_head(column, 2), by_head(column, 4), [bests[0], *parts]
        )
        bests.append(best_of(along_x))
        bests.append(best_of(along_y, bests[1:]))
        across = stack([by_head(along_y_half, 2), by_head(along_x_half, 4)], bests[2:])
        bests.append(best_of(across))
    else:
        for s in range(1, chips):
            bests.append(best_of(by_head(column, 2 * s), bests[-1:]))
    sums = out_layer(*join(own_two, parts))
    (hiddens,) = finish_layer(True, sums, residual_two)

    best = gather_best(place, square, bests)
    is_max = lax.broadcasted_iota(jnp.int32, best.shape, 0) < chips
    for axis, size in (("head", head_count), ("tok", tok_count)):
        mask = 1
        while mask < size:
            other = lax.ppermute(best, axis, xor_pairs(size, mask))
            best = jnp.where(is_max, jnp.maximum(best, other), best + other)
            mask *= 2
    top_logits = best[:chips].reshape(chips, tok_count, 2, share).transpose(1, 0, 2, 3).reshape(-1)
    request_norms = jnp.sqrt(best[chips, :tok_count] / (block_rows * model_width))
    return (hiddens, request_norms, top_logits)


def solution(mesh):
    placed = (
        P("tok", "head"),
        P(),
        P("tok"),
        P(),
        P("tok", "head"),
        P("tok", "head"),
        P(None, "head"),
        P(None, "head"),
        P(None, "head"),
        P("head", None),
        P(),
        P(),
        P("tok", "head"),
        P(("tok", "head"), None),
    )
    return jax.shard_map(
        shards,
        mesh=mesh,
        in_specs=placed,
        out_specs=(P(("tok", "head"), None), P(), P()),
        check_vma=False,
    )
```

```python
import functools
import math

import jax
import jax.numpy as jnp
from jax import lax
from jax.experimental import pallas as pl
from jax.experimental.pallas import tpu as pltpu
from jax.sharding import PartitionSpec as P

HEAD_DIM = 128
EPSILON = 1e-06
LOWEST = -1e30
BF16 = jnp.bfloat16
F32 = jnp.float32

SMEM = pl.BlockSpec(memory_space=pltpu.SMEM)
VMEM = pl.BlockSpec(memory_space=pltpu.VMEM)
HBM = pl.BlockSpec(memory_space=pltpu.HBM)


def params(mib=24):
    return pltpu.CompilerParams(vmem_limit_bytes=mib * 2**20)


def cost(flops, moved):
    return pl.CostEstimate(flops=flops, bytes_accessed=moved, transcendentals=0)


def call(kernel, operands, after=(), in_specs=None, **rest):
    count = len(operands)

    def body(*refs):
        kernel(*refs[:count], *refs[count + len(after) :])

    specs = list(in_specs) + [pl.BlockSpec(memory_space=pl.ANY)] * len(after)
    return pl.pallas_call(body, in_specs=specs, **rest)(*operands, *after)


def xor_pairs(size, mask):
    return [(i, i ^ mask) for i in range(size)]


def fetch(sources, targets, sems):
    copies = [pltpu.make_async_copy(a, b, sems.at[i]) for i, (a, b) in enumerate(zip(sources, targets, strict=True))]
    for copy in copies:
        copy.start()
    return copies


def carry_kernel(*refs):
    count = len(refs) // 2
    for source, out in zip(refs[:count], refs[count:], strict=True):
        out[...] = source[...]


def carry(*arrays):
    return pl.pallas_call(
        carry_kernel,
        out_shape=tuple(jax.ShapeDtypeStruct(a.shape, a.dtype) for a in arrays),
        in_specs=[VMEM] * len(arrays),
        out_specs=(VMEM,) * len(arrays),
        compiler_params=params(),
        name="carry",
    )(*arrays)


def first_kernel(place, *refs):
    project_kernel(place, *refs[:-5], refs[-1])
    for source, out in zip((refs[0], *refs[-12:-9]), refs[-5:-1], strict=True):
        out[...] = source[...]


def project_kernel(place, *refs):
    *pieces, wq, wk, wv, q_out, k_out, v_out, res_out, x = refs
    head = place[1]
    rows, width = q_out.shape
    for odd in range(2):
        mask = odd
        for piece in pieces[odd * len(pieces) // 2 : (odd + 1) * len(pieces) // 2]:
            for start in range(0, piece.shape[0], rows):
                at = pl.multiple_of(jnp.bitwise_xor(head, mask) * width, width)
                x[:, pl.ds(at, width)] = piece[start : start + rows, :]
                mask += 2
    for w, out in ((wq, q_out), (wk, k_out), (wv, v_out)):
        out[...] = jnp.dot(x[...], w[...], preferred_element_type=F32).astype(BF16)
    share = res_out.shape[0]
    res_out[...] = x[pl.ds(pl.multiple_of(head * share, share), share), :]


def project(rows, place, pieces, wq, wk, wv, after=()):
    full, width = wq.shape
    share = rows // (full // width)
    tile = jax.ShapeDtypeStruct((rows, width), BF16)
    return call(
        first_kernel,
        (place, *pieces, wq, wk, wv),
        after,
        out_shape=(tile, tile, tile, jax.ShapeDtypeStruct((share, full), BF16), tile) + (jax.ShapeDtypeStruct(wq.shape, BF16),) * 3,
        in_specs=[SMEM] + [VMEM] * (len(pieces) + 3),
        out_specs=(VMEM,) * 8,
        scratch_shapes=[pltpu.VMEM((rows, full), BF16)],
        compiler_params=params(),
        cost_estimate=cost(6 * rows * full * width, 8 * full * width),
        name="project",
    )


def key_range(place, request, chunk, chunk_rows, tok_count):
    begin = jnp.int32(0)
    length = jnp.int32(0)
    for i in range(tok_count):
        begin += jnp.where(i < request, place[2 + i], 0)
        length += jnp.where(i == request, place[2 + i], 0)
    begin -= chunk * chunk_rows
    low = jnp.clip(begin, 0, chunk_rows)
    high = jnp.clip(begin + length, 0, chunk_rows)
    return low, high


def absorb(state, query, keys, values, valid):
    top, acc = state
    factor = math.log2(math.e) / math.sqrt(HEAD_DIM)
    scores = lax.dot_general(query, keys, (((1,), (1,)), ((), ())), preferred_element_type=F32)
    if valid is not None:
        scores = jnp.where(valid, scores, LOWEST)
    new_top = jnp.maximum(top, jnp.max(scores, axis=1, keepdims=True))
    weights = jnp.exp2((scores - new_top) * factor).astype(BF16)
    wide = jnp.concatenate([values, jnp.ones_like(values)], axis=1)
    acc = acc * jnp.exp2((top - new_top) * factor) + jnp.dot(weights, wide, preferred_element_type=F32)
    return new_top, acc


def cached_states(place, request, query, keys, values, tok_count):
    rows, width = query.shape
    chunk_rows = keys.shape[0]
    heads = width // HEAD_DIM
    span = min(512, chunk_rows)
    low, high = key_range(place, request, place[0], chunk_rows, tok_count)
    first = low // span
    last = jnp.where(high > low, (high + span - 1) // span, first)

    def step(block, states):
        start = pl.multiple_of(block * span, span)
        spots = start + lax.broadcasted_iota(jnp.int32, (rows, span), 1)
        valid = (spots >= low) & (spots < high)
        out = []
        for j in range(heads):
            cols = slice(j * HEAD_DIM, (j + 1) * HEAD_DIM)
            out.append(
                absorb(states[j], query[:, cols], keys[pl.ds(start, span), cols], values[pl.ds(start, span), cols], valid)
            )
        return tuple(out)

    empty = (jnp.full((rows, 1), LOWEST, F32), jnp.zeros((rows, 2 * HEAD_DIM), F32))
    return lax.fori_loop(first, last, step, (empty,) * heads)


def settle(state):
    top, acc = state
    total = acc[:, HEAD_DIM:]
    some = total > 0.0
    safe = jnp.where(some, total, 1.0)
    log_sum = jnp.where(some, top * (1.0 / math.sqrt(HEAD_DIM)) + jnp.log(safe), LOWEST)
    return acc[:, :HEAD_DIM] / safe, log_sum


def own_kernel(tok_count, place, query, new_keys, new_values, keys, values, mixed_out, log_out):
    states = cached_states(place, place[0], query, keys, values, tok_count)
    for j, state in enumerate(states):
        cols = slice(j * HEAD_DIM, (j + 1) * HEAD_DIM)
        state = absorb(state, query[:, cols], new_keys[:, cols], new_values[:, cols], None)
        mixed, log_sum = settle(state)
        mixed_out[:, cols] = mixed
        log_out[:, cols] = log_sum


def own_part(tok_count, place, query, new_keys, new_values, keys, values, after=()):
    rows, width = query.shape
    shape = jax.ShapeDtypeStruct((rows, width), F32)
    return call(
        functools.partial(own_kernel, tok_count),
        (place, query, new_keys, new_values, keys, values),
        after,
        out_shape=(shape, shape),
        in_specs=[SMEM] + [VMEM] * 5,
        out_specs=(VMEM, VMEM),
        compiler_params=params(),
        cost_estimate=cost(4 * rows * width * keys.shape[0], 4 * keys.shape[0] * width),
        name="own_part",
    )


def away_part(place, mask, query, keys, values, out, tok_count):
    rows, width = query.shape
    states = cached_states(place, jnp.bitwise_xor(place[0], mask), query, keys, values, tok_count)
    pieces = []
    for j, state in enumerate(states):
        mixed, log_sum = settle(state)
        out[:rows, j * HEAD_DIM : (j + 1) * HEAD_DIM] = mixed.astype(BF16)
        rest = jnp.transpose(log_sum)[:1, :]
        for _ in range(3):
            piece = rest.astype(BF16).astype(F32)
            pieces.append(piece)
            rest = rest - piece
    at = lax.broadcasted_iota(jnp.int32, (16, rows), 0)
    tail = jnp.zeros((16, rows), F32)
    for i, piece in enumerate(pieces):
        tail = jnp.where(at == i, piece, tail)
    out[rows : rows + 16, :] = tail.astype(BF16)


def second_kernel(tok_count, masks, place, *refs):
    count = len(masks)
    queries, (keys, values), refs = refs[:count], refs[count : count + 2], refs[count + 2 :]
    messages, x = refs[-5 - count : -5], refs[-1]
    project_kernel(place, *refs[: -5 - count], *refs[-5:-1], x)
    for mask, query, message in zip(masks, queries, messages, strict=True):
        away_part(place, mask, query, keys, values, message, tok_count)


def second_stage(tok_count, masks, place, queries, keys, values, pieces, wq, wk, wv, after=()):
    rows, width = queries[0].shape
    full = wq.shape[0]
    share = rows // (full // width)
    tile = jax.ShapeDtypeStruct((rows, width), BF16)
    message = jax.ShapeDtypeStruct((rows + 16, width), BF16)
    outs = (message,) * len(masks) + (tile, tile, tile, jax.ShapeDtypeStruct((share, full), BF16))
    results = call(
        functools.partial(second_kernel, tok_count, masks),
        (place, *queries, keys, values, *pieces, wq, wk, wv),
        after,
        out_shape=outs,
        in_specs=[SMEM] + [VMEM] * (len(masks) + len(pieces) + 5),
        out_specs=(VMEM,) * len(outs),
        scratch_shapes=[pltpu.VMEM((rows, full), BF16)],
        compiler_params=params(),
        cost_estimate=cost(4 * rows * width * keys.shape[0] + 6 * rows * full * width, 8 * full * width),
        name="second_stage",
    )
    return results[: len(masks)], results[len(masks) :]


def away_kernel(tok_count, masks, place, *refs):
    count = len(masks)
    queries, (keys, values), outs = refs[:count], refs[count : count + 2], refs[count + 2 :]
    for mask, query, out in zip(masks, queries, outs, strict=True):
        away_part(place, mask, query, keys, values, out, tok_count)


def away_parts(tok_count, masks, place, queries, keys, values, after=()):
    rows, width = queries[0].shape
    out = jax.ShapeDtypeStruct((rows + 16, width), BF16)
    return call(
        functools.partial(away_kernel, tok_count, masks),
        (place, *queries, keys, values),
        after,
        out_shape=(out,) * len(masks),
        in_specs=[SMEM] + [VMEM] * (len(masks) + 2),
        out_specs=(VMEM,) * len(masks),
        compiler_params=params(),
        cost_estimate=cost(4 * rows * width * keys.shape[0], 4 * keys.shape[0] * width),
        name="away_parts",
    )


def combine_kernel(share, place, mixed, logs, *refs):
    *messages, keep_out, send_out, whole = refs
    rows, width = mixed.shape
    tails = [message[rows : rows + 16, :].astype(F32) for message in messages]
    for j in range(width // HEAD_DIM):
        cols = slice(j * HEAD_DIM, (j + 1) * HEAD_DIM)
        parts = [(mixed[:, cols], logs[:, cols])]
        for message, tail in zip(messages, tails, strict=True):
            row = tail[3 * j : 3 * j + 1] + tail[3 * j + 1 : 3 * j + 2] + tail[3 * j + 2 : 3 * j + 3]
            log_sum = jnp.transpose(jnp.broadcast_to(row, (HEAD_DIM, rows)))
            parts.append((message[:rows, cols].astype(F32), log_sum))
        top = functools.reduce(jnp.maximum, [log_sum for _, log_sum in parts])
        total, acc = 0.0, 0.0
        for part, log_sum in parts:
            weight = jnp.exp(log_sum - top)
            total += weight
            acc += weight * part
        whole[:, cols] = (acc / total).astype(BF16)
    head = place[1]
    core = jnp.bitwise_and(head, 1)
    for slot in range(keep_out.shape[0] // share):
        pair = jnp.bitwise_xor(head, 2 * slot) - core
        at = pl.multiple_of((pair + core) * share, share)
        other = pl.multiple_of((pair + 1 - core) * share, share)
        keep_out[slot * share : (slot + 1) * share, :] = whole[pl.ds(at, share), :]
        send_out[slot * share : (slot + 1) * share, :] = whole[pl.ds(other, share), :]


def combine(share, place, mixed, logs, messages, after=()):
    rows, width = mixed.shape
    half = jax.ShapeDtypeStruct((rows // 2, width), BF16)
    return call(
        functools.partial(combine_kernel, share),
        (place, mixed, logs, *messages),
        after,
        out_shape=(half, half),
        in_specs=[SMEM] + [VMEM] * (len(messages) + 2),
        out_specs=(VMEM, VMEM),
        scratch_shapes=[pltpu.VMEM((rows, width), BF16)],
        compiler_params=params(),
        cost_estimate=cost(rows * width * 40, rows * width * 16),
        name="combine",
    )


def ids_kernel(tok_count, vocab_here, place, ids, local_out, owner_out):
    tiles = ids.shape[0] // tok_count
    for slot in range(tok_count):
        for tile in range(tiles):
            row = ids[pl.ds(jnp.bitwise_xor(place[0], slot) * tiles + tile, 1), :]
            at = slot * tiles + tile
            local_out[at : at + 1, :] = jnp.clip(row - place[0] * vocab_here, 0, vocab_here - 1)
            if slot == 0:
                owner = jnp.zeros(row.shape, jnp.int32)
                for i in range(1, tok_count):
                    owner += jnp.where(row >= i * vocab_here, 1, 0)
                owner_out[:, tile * 128 : (tile + 1) * 128] = owner


def sort_ids(tok_count, vocab_here, place, ids):
    ids = ids.reshape(-1, 128)
    local, owner = pl.pallas_call(
        functools.partial(ids_kernel, tok_count, vocab_here),
        out_shape=(
            jax.ShapeDtypeStruct(ids.shape, jnp.int32),
            jax.ShapeDtypeStruct((1, ids.size // tok_count), jnp.int32),
        ),
        in_specs=[SMEM, VMEM],
        out_specs=(VMEM, VMEM),
        compiler_params=params(),
        name="sort_ids",
    )(place, ids)
    return local.reshape(-1), owner


def choose_kernel(place, accept, owner, states, *refs):
    *found, out = refs
    rows = states.shape[0]
    slot = jnp.where(accept[...] == 1, jnp.bitwise_xor(owner[...], place[0]), len(found)).astype(F32)
    slot = jnp.transpose(jnp.broadcast_to(slot, (128, rows)))
    for start in range(0, states.shape[1], 128):
        cols = slice(start, start + 128)
        value = states[:, cols].astype(F32)
        for i, rows_found in enumerate(found):
            value = jnp.where(slot == i, rows_found[:, cols].astype(F32), value)
        out[:, cols] = value.astype(BF16)


def choose(place, accept, owner, states, found, after=()):
    return call(
        choose_kernel,
        (place, accept, owner, states, *found),
        after,
        out_shape=jax.ShapeDtypeStruct(states.shape, BF16),
        in_specs=[SMEM] + [VMEM] * (3 + len(found)),
        out_specs=VMEM,
        compiler_params=params(),
        name="choose",
    )


def stack_kernel(*refs):
    *pieces, out = refs
    at = 0
    for piece in pieces:
        out[at : at + piece.shape[0], :] = piece[...]
        at += piece.shape[0]


def stack(pieces, after=()):
    rows = sum(piece.shape[0] for piece in pieces)
    return call(
        stack_kernel,
        tuple(pieces),
        after,
        out_shape=jax.ShapeDtypeStruct((rows, pieces[0].shape[1]), BF16),
        in_specs=[VMEM] * len(pieces),
        out_specs=VMEM,
        compiler_params=params(),
        name="stack",
    )


def out_kernel(keep, other, w_keep, w_other, *outs):
    share = outs[0].shape[0]
    total = jnp.dot(other[...], w_other[...], preferred_element_type=F32)
    total += jnp.dot(keep[...], w_keep[...], preferred_element_type=F32)
    for slot, out in enumerate(outs):
        out[...] = total[slot * share : (slot + 1) * share].astype(out.dtype)


def out_project(share, keep, other, w_keep, w_other):
    half, width = keep.shape
    full = w_keep.shape[1]
    return pl.pallas_call(
        out_kernel,
        out_shape=tuple(jax.ShapeDtypeStruct((share, full), F32 if s == 0 else BF16) for s in range(half // share)),
        in_specs=[VMEM] * 4,
        out_specs=(VMEM,) * (half // share),
        compiler_params=params(),
        cost_estimate=cost(4 * half * width * full, 4 * width * full),
        name="out_project",
    )(keep, other, w_keep, w_other)


def finish_kernel(last, own, *refs):
    *refs, attn_gain, final_gain, sems = refs
    *others, residual, attn_far, final_far, first_out = refs[: len(refs) - (0 if last else 2)]
    copies = fetch((attn_far, final_far), (attn_gain, final_gain), sems)
    total = own[...]
    for other in others:
        total += other[...].astype(F32)
    scale = lax.rsqrt(jnp.mean(total * total, axis=1, keepdims=True) + EPSILON)
    for copy in copies:
        copy.wait()
    first = (residual[...].astype(F32) + total * scale * attn_gain[...]).astype(BF16)
    first_out[...] = first
    if not last:
        normed_out, square_out = refs[-2:]
        wide = first.astype(F32)
        squares = jnp.sum(wide * wide, axis=1, keepdims=True)
        scale = lax.rsqrt(squares / wide.shape[1] + EPSILON)
        normed_out[...] = (wide * scale * final_gain[...]).astype(BF16)
        square_out[...] = jnp.broadcast_to(jnp.sum(squares, axis=0, keepdims=True), square_out.shape)


def finish(last, own, others, residual, attn_gain, final_gain, after=()):
    state = jax.ShapeDtypeStruct(residual.shape, BF16)
    outs = (state,) if last else (state, state, jax.ShapeDtypeStruct((1, 128), F32))
    return call(
        functools.partial(finish_kernel, last),
        (own, *others, residual, attn_gain, final_gain),
        after,
        out_shape=outs,
        in_specs=[VMEM] * (len(others) + 2) + [HBM] * 2,
        out_specs=(VMEM,) * len(outs),
        scratch_shapes=[pltpu.VMEM(attn_gain.shape, F32)] * 2 + [pltpu.SemaphoreType.DMA((2,))],
        compiler_params=params(),
        cost_estimate=cost(residual.size * 20, residual.size * 12),
        name="finish",
    )


def hand_on_kernel(first, second, *outs):
    half = first.shape[0] // 2
    outs[0][...] = first[...]
    outs[1][...] = second[...]
    outs[2][...] = second[:half, :]
    outs[3][...] = first[half:, :]


def hand_on(first, second, after=()):
    whole = jax.ShapeDtypeStruct(first.shape, BF16)
    half = jax.ShapeDtypeStruct((first.shape[0] // 2, first.shape[1]), BF16)
    return call(
        hand_on_kernel,
        (first, second),
        after,
        out_shape=(whole, whole, half, half),
        in_specs=[VMEM] * 2,
        out_specs=(VMEM,) * 4,
        compiler_params=params(),
        name="hand_on",
    )


def logits_kernel(share, tok_count, place, mine, other, lm_block, best_out, x):
    @pl.when(pl.program_id(0) == 0)
    def _():
        core = jnp.bitwise_and(place[1], 1)
        for flag, piece in enumerate((mine, other)):
            for slot in range(tok_count):
                tok = jnp.bitwise_xor(place[0], slot)
                at = pl.multiple_of((2 * tok + jnp.bitwise_xor(core, flag)) * share, share)
                x[pl.ds(at, share), :] = piece[slot * share : (slot + 1) * share, :]
        best_out[...] = jnp.full(best_out.shape, -jnp.inf, F32)

    logits = lax.dot_general(lm_block[...], x[...], (((1,), (1,)), ((), ())), preferred_element_type=F32)
    best = jnp.max(logits.reshape(logits.shape[0] // 8, 8, logits.shape[1]), axis=0)
    best_out[...] = jnp.maximum(best_out[...], best)


def largest_logits(share, tok_count, place, mine, other, lm_head, after=()):
    half, full = mine.shape
    vocab = lm_head.shape[0]
    span = vocab // 2 if vocab % 32 == 0 else vocab // 7
    return call(
        functools.partial(logits_kernel, share, tok_count),
        (place, mine, other, lm_head),
        after,
        out_shape=jax.ShapeDtypeStruct((8, 2 * half), F32),
        grid=(vocab // span,),
        in_specs=[SMEM, VMEM, VMEM, pl.BlockSpec((span, full), lambda i: (i, 0))],
        out_specs=VMEM,
        scratch_shapes=[pltpu.VMEM((2 * half, full), BF16)],
        compiler_params=params(),
        cost_estimate=cost(4 * half * full * vocab, 2 * full * vocab),
        name="largest_logits",
    )


def gather_best_kernel(place, square, *refs):
    *bests, out = refs
    chip = place[1] // 2
    out[...] = jnp.zeros(out.shape, F32)
    for slot, best in enumerate(bests):
        out[pl.ds(jnp.bitwise_xor(chip, slot), 1), :] = jnp.max(best[...], axis=0, keepdims=True)
    lanes = lax.broadcasted_iota(jnp.int32, (1, out.shape[1]), 1)
    out[len(bests) : len(bests) + 1, :] = jnp.where(lanes == place[0], square[:, :1], 0.0)


def gather_best(place, square, bests):
    rows = -(-(len(bests) + 1) // 8) * 8
    return pl.pallas_call(
        gather_best_kernel,
        out_shape=jax.ShapeDtypeStruct((rows, bests[0].shape[1]), F32),
        in_specs=[SMEM] + [VMEM] * (1 + len(bests)),
        out_specs=VMEM,
        compiler_params=params(),
        name="gather_best",
    )(place, square, *bests)


def shards(
    block_states,
    token_ids,
    accept,
    cache_lengths,
    cache_keys,
    cache_values,
    w_query,
    w_key,
    w_value,
    w_out,
    attn_gain,
    final_gain,
    embed,
    lm_head,
):
    tok_index = lax.axis_index("tok")
    head_index = lax.axis_index("head")
    tok_count = lax.axis_size("tok")
    head_count = lax.axis_size("head")
    chips = head_count // 2
    block_rows = block_states.shape[0]
    share = block_rows // head_count
    model_width = w_query.shape[0]
    place = jnp.concatenate([jnp.stack([tok_index, head_index]).astype(jnp.int32), cache_lengths])
    gains = (attn_gain.reshape(1, -1), final_gain.reshape(1, -1))
    tok_masks = range(1, tok_count)

    def by_head(value, mask):
        return lax.ppermute(value, "head", xor_pairs(head_count, mask))

    def by_tok(value, mask):
        return lax.ppermute(value, "tok", xor_pairs(tok_count, mask))

    def spread(features):
        pieces = [features] + [by_head(features, 2 * s) for s in range(1, chips)]
        return pieces, [by_head(piece, 1) for piece in pieces]

    def exchange(arrays):
        return [by_tok(array, mask) for mask, array in zip(tok_masks, arrays, strict=True)]

    def join(own, messages, after=()):
        return combine(share, place, *own, messages, after)

    def out_layer(keep, send):
        return out_project(share, keep, by_head(send, 1), w_out, w_out_other)

    def finish_layer(last, sums, residual, after=()):
        own, *others = sums
        others = [by_head(total, 2 * s) for s, total in enumerate(others, 1)]
        return finish(last, own, others, residual, *gains, after)


    w_out_other = by_head(w_out, 1)

    vocab_here = embed.shape[0]
    ids, owners = sort_ids(tok_count, vocab_here, place, token_ids)
    found = embed.at[ids].get(mode="promise_in_bounds").reshape(tok_count, block_rows, -1)
    found = [found[mask] for mask in range(tok_count)]
    embedded = [found[0], *exchange(found[1:])]

    pieces, others = spread(block_states)
    query, key, value, residual, states, *weights = project(
        block_rows, place, pieces + others, w_query, w_key, w_value, [w_out_other, found[1]]
    )
    queries = exchange([query] * len(tok_masks))
    cache_keys, cache_values, accepted = carry(cache_keys, cache_values, accept.reshape(1, -1))
    own = own_part(tok_count, place, query, key, value, cache_keys, cache_values)
    chosen = choose(place, accepted, owners, states, embedded, queries[:1])
    pieces, others = spread(chosen)
    messages, (query, key, value, residual_two) = second_stage(
        tok_count, tok_masks, place, queries, cache_keys, cache_values, pieces + others, *weights
    )
    messages = exchange(messages)
    queries = exchange([query] * len(tok_masks))
    own_two = own_part(tok_count, place, query, key, value, cache_keys, cache_values)
    keep = join(own, messages, [own_two[0], queries[0]])
    parts = away_parts(tok_count, tok_masks, place, queries, cache_keys, cache_values, [keep[0]])
    _, normed, square = finish_layer(False, out_layer(*keep), residual)

    column = stack([normed] + exchange([normed] * len(tok_masks)), parts[:1])
    parts = exchange(parts)

    def best_of(piece, after=()):
        return largest_logits(share, tok_count, place, piece, by_head(piece, 1), lm_head, after)

    bests = [best_of(column)]
    if chips == 4:
        along_x, along_y, along_y_half, along_x_half = hand_on(
            by_head(column, 2), by_head(column, 4), [bests[0], *parts]
        )
        bests.append(best_of(along_x))
        bests.append(best_of(along_y, bests[1:]))
        across = stack([by_head(along_y_half, 2), by_head(along_x_half, 4)], bests[2:])
        bests.append(best_of(across))
    else:
        for s in range(1, chips):
            bests.append(best_of(by_head(column, 2 * s), bests[-1:]))
    sums = out_layer(*join(own_two, parts))
    (hiddens,) = finish_layer(True, sums, residual_two)

    best = gather_best(place, square, bests)
    is_max = lax.broadcasted_iota(jnp.int32, best.shape, 0) < chips
    for axis, size in (("head", head_count), ("tok", tok_count)):
        mask = 1
        while mask < size:
            other = lax.ppermute(best, axis, xor_pairs(size, mask))
            best = jnp.where(is_max, jnp.maximum(best, other), best + other)
            mask *= 2
    top_logits = best[:chips].reshape(chips, tok_count, 2, share).transpose(1, 0, 2, 3).reshape(-1)
    request_norms = jnp.sqrt(best[chips, :tok_count] / (block_rows * model_width))
    return (hiddens, request_norms, top_logits)


def solution(mesh):
    placed = (
        P("tok", "head"),
        P(),
        P("tok"),
        P(),
        P("tok", "head"),
        P("tok", "head"),
        P(None, "head"),
        P(None, "head"),
        P(None, "head"),
        P("head", None),
        P(),
        P(),
        P("tok", "head"),
        P(("tok", "head"), None),
    )
    return jax.shard_map(
        shards,
        mesh=mesh,
        in_specs=placed,
        out_specs=(P(("tok", "head"), None), P(), P()),
        check_vma=False,
    )
```
